32 devices in a mesh: fsdp: 4 (over z), ctx: 4 (over x, core), tp: 2 (over y).
Axes of the slice: x: 2, y: 2, z: 4, core: 2. Of those that a mesh axis runs over, the one named last changes fastest.
Arguments:
- residual: bfloat16 [8192, 2048], P(('fsdp', 'ctx')), may hold values from -6 to 6
- cotangent: bfloat16 [8192, 2048], P(('fsdp', 'ctx')), may hold values from -6 to 6
- lengths: int32 [4, 4], P('fsdp'), may hold values from 1 to 1024, 2048 in all within a row
- token_order: int32 [4, 2048], P('fsdp'), may hold values from 0 to 2047, each once within a row
- norm_mixer: bfloat16 [2048], P(('fsdp', 'ctx')), may hold values from 0.5 to 1.5
- w_query: bfloat16 [2048, 2048], P(('fsdp', 'ctx'), 'tp'), may hold values from -0.125 to 0.125
- w_key: bfloat16 [2048, 2048], P(('fsdp', 'ctx'), 'tp'), may hold values from -0.125 to 0.125
- w_value: bfloat16 [2048, 4096], P(('fsdp', 'ctx'), 'tp'), may hold values from -0.125 to 0.125
- w_outgate: bfloat16 [2048, 4096], P(('fsdp', 'ctx'), 'tp'), may hold values from -0.125 to 0.125
- w_decay: bfloat16 [2048, 16], P(('fsdp', 'ctx'), 'tp'), may hold values from -0.125 to 0.125
- w_beta: bfloat16 [2048, 16], P(('fsdp', 'ctx'), 'tp'), may hold values from -0.125 to 0.125
- conv_query: bfloat16 [4, 2048], replicated, may hold values from -3 to 3
- conv_key: bfloat16 [4, 2048], replicated, may hold values from -3 to 3
- conv_value: bfloat16 [4, 4096], replicated, may hold values from -3 to 3
- decay_log: float32 [16], replicated, may hold values from -1.5 to 1
- decay_bias: float32 [16], replicated, may hold values from -4 to -1
- norm_head: bfloat16 [256], replicated, may hold values from 0.5 to 1.5
- w_output: bfloat16 [4096, 2048], P('tp', ('fsdp', 'ctx')), may hold values from -0.125 to 0.125
- norm_ffn: bfloat16 [2048], P(('fsdp', 'ctx')), may hold values from 0.5 to 1.5
- w_gate: bfloat16 [2048, 5632], P(('fsdp', 'ctx'), 'tp'), may hold values from -0.125 to 0.125
- w_up: bfloat16 [2048, 5632], P(('fsdp', 'ctx'), 'tp'), may hold values from -0.125 to 0.125
- w_down: bfloat16 [5632, 2048], P('tp', ('fsdp', 'ctx')), may hold values from -0.078125 to 0.078125
Outputs:
- output: bfloat16 [8192, 2048], P(('fsdp', 'ctx'))
- grad_input: bfloat16 [8192, 2048], P(('fsdp', 'ctx'))
- gnorm_mixer: float32 [2048], P(('fsdp', 'ctx'))
- gw_query: float32 [2048, 2048], P(('fsdp', 'ctx'), 'tp')
- gw_key: float32 [2048, 2048], P(('fsdp', 'ctx'), 'tp')
- gw_value: float32 [2048, 4096], P(('fsdp', 'ctx'), 'tp')
- gw_outgate: float32 [2048, 4096], P(('fsdp', 'ctx'), 'tp')
- gw_decay: float32 [2048, 16], P(('fsdp', 'ctx'), 'tp')
- gw_beta: float32 [2048, 16], P(('fsdp', 'ctx'), 'tp')
- gconv_query: float32 [4, 2048], replicated
- gconv_key: float32 [4, 2048], replicated
- gconv_value: float32 [4, 4096], replicated
- gdecay_log: float32 [16], replicated
- gdecay_bias: float32 [16], replicated
- gnorm_head: float32 [256], replicated
- gw_output: float32 [4096, 2048], P('tp', ('fsdp', 'ctx'))
- gnorm_ffn: float32 [2048], P(('fsdp', 'ctx'))
- gw_gate: float32 [2048, 5632], P(('fsdp', 'ctx'), 'tp')
- gw_up: float32 [2048, 5632], P(('fsdp', 'ctx'), 'tp')
- gw_down: float32 [5632, 2048], P('tp', ('fsdp', 'ctx'))
The draws below stay inside these ranges and needn't reach their ends.
Inputs may be any that keep to these rules, and one draw needn't show every extreme that they name: Each row of lengths holds the lengths of the 4 sequences of one group; they sum to 2048. Each row of token_order is a permutation of the 2048 rows of one group.
All inputs are finite; a program needn't handle non-finite values.
Results may differ from the reference program's by a relative error of at most 0.017.
Values may be sent and summed in bfloat16 or wider, within the bound.
No kernel may reach another device: no remote copies, remote signals or barrier semaphores. Data moves between devices by JAX's collectives and lax.ppermute only.
A program may use at most 320 MiB of HBM per device.

```python
import math
import jax
import jax.numpy as jnp
import numpy as np
from jax import lax

D = 2048
HEADS = 16
DV = 256
FF = 5632
KERNEL = 4
SPAN = 64
MAXLEN = 1024
SEQS = 4
HK = 2048
HV = 4096
GROUP = 2048
TOKENS = 8192
N_FSDP = 4


def level_of(rng, dims, split, smallest, top_value):
    def one(axis_at, shards_of):
        draws = jax.random.uniform(jax.random.fold_in(jax.random.fold_in(rng, 6), axis_at), (shards_of,), jnp.float32, smallest / len(split), top_value / len(split))
        return jnp.repeat(jnp.exp(draws), dims[axis_at] // shards_of).reshape((-1,) + (1,) * (len(dims) - axis_at - 1))

    loudness = one(*split[0])
    for cut in split[1:]:
        loudness = loudness * one(*cut)
    return loudness


def profile(amount, total, most, lean):
    portions = [(1 << 20) // math.isqrt(grade ** lean) + 1 for grade in range(2, amount + 1)]
    spare, given = total - most - (amount - 1), [1] * (amount - 1)
    while spare > 0:
        candidates = [i for i in range(amount - 1) if given[i] < most]
        whole, budget = sum([portions[i] for i in candidates]), spare
        for i in candidates:
            more = min(most - given[i], max(1, budget * portions[i] // whole), spare)
            given[i] = given[i] + more
            spare = spare - more
    return np.array([most] + given)


def ragged_sizes(key, count, total, bound, skew):
    if count == 2:
        one = jax.random.randint(key, (), max(1, total - bound), min(bound, total - 1) + 1)
        return jnp.stack([one, total - one])
    sizes = jnp.asarray(profile(count, total, bound, skew), jnp.int32)
    twos = (count - 1) // 2
    source_of, taker = sizes[1:1 + 2 * twos:2], sizes[2:2 + 2 * twos:2]
    slack = jnp.minimum(source_of - 1, bound - taker)
    passed = jax.random.randint(jax.random.fold_in(key, 1), (twos,), 0, 1 << 20) % (slack + 1)
    sizes = sizes.at[1:1 + 2 * twos:2].set(source_of - passed).at[2:2 + 2 * twos:2].set(taker + passed)
    return sizes[jax.random.permutation(jax.random.fold_in(key, 2), count)]


def scatter_about(key, shape, deviation, bound, cuts=(), kind=jnp.bfloat16):
    factor_of = level_of(key, shape, cuts, -0.22, 0.18) if cuts else 1.0
    entries = jax.random.normal(key, shape, jnp.float32) * deviation * factor_of
    return jnp.minimum(jnp.maximum(entries, -bound), bound).astype(kind)


def setup_inputs(seed: int = 0) -> dict:
    arg_keys = jax.random.split(jax.random.key(seed), 23)
    return {
        "residual": scatter_about(arg_keys[0], (TOKENS, D), 1.0, 6.0, ((0, 16),)),
        "cotangent": scatter_about(arg_keys[1], (TOKENS, D), 1.0, 6.0, ((0, 16),)),
        "lengths": jax.vmap(lambda own: ragged_sizes(own, SEQS, GROUP, MAXLEN, 2))(jax.random.split(arg_keys[2], N_FSDP)).reshape((N_FSDP, SEQS)).astype(jnp.int32),
        "token_order": jax.vmap(lambda own: jax.random.permutation(own, GROUP))(jax.random.split(arg_keys[3], N_FSDP)).reshape((N_FSDP, GROUP)).astype(jnp.int32),
        "norm_mixer": jnp.clip(1.0 + 0.1 * jax.random.normal(arg_keys[4], (D,), jnp.float32), 0.5, 1.5).astype(jnp.bfloat16),
        "w_query": scatter_about(arg_keys[5], (D, HK), D ** -0.5, 0.125, ((0, 16), (1, 2))),
        "w_key": scatter_about(arg_keys[6], (D, HK), D ** -0.5, 0.125, ((0, 16), (1, 2))),
        "w_value": scatter_about(arg_keys[7], (D, HV), D ** -0.5, 0.125, ((0, 16), (1, 2))),
        "w_outgate": scatter_about(arg_keys[8], (D, HV), D ** -0.5, 0.125, ((0, 16), (1, 2))),
        "w_decay": scatter_about(arg_keys[9], (D, HEADS), D ** -0.5, 0.125, ((0, 16), (1, 2))),
        "w_beta": scatter_about(arg_keys[10], (D, HEADS), D ** -0.5, 0.125, ((0, 16), (1, 2))),
        "conv_query": scatter_about(arg_keys[11], (KERNEL, HK), KERNEL ** -0.5, 3.0),
        "conv_key": scatter_about(arg_keys[12], (KERNEL, HK), KERNEL ** -0.5, 3.0),
        "conv_value": scatter_about(arg_keys[13], (KERNEL, HV), KERNEL ** -0.5, 3.0),
        "decay_log": jnp.clip(jax.random.uniform(arg_keys[14], (HEADS,), jnp.float32, -1.5, 1.0), -1.5, 1.0),
        "decay_bias": jnp.clip(jax.random.uniform(arg_keys[15], (HEADS,), jnp.float32, -4.0, -1.0), -4.0, -1.0),
        "norm_head": jnp.clip(1.0 + 0.1 * jax.random.normal(arg_keys[16], (DV,), jnp.float32), 0.5, 1.5).astype(jnp.bfloat16),
        "w_output": scatter_about(arg_keys[17], (HV, D), (HV // 2) ** -0.5, 0.125, ((0, 2), (1, 16))),
        "norm_ffn": jnp.clip(1.0 + 0.1 * jax.random.normal(arg_keys[18], (D,), jnp.float32), 0.5, 1.5).astype(jnp.bfloat16),
        "w_gate": scatter_about(arg_keys[19], (D, FF), D ** -0.5, 0.125, ((0, 16), (1, 2))),
        "w_up": scatter_about(arg_keys[20], (D, FF), D ** -0.5, 0.125, ((0, 16), (1, 2))),
        "w_down": scatter_about(arg_keys[21], (FF, D), FF ** -0.5, 0.078125, ((0, 2), (1, 16))),
    }


EPS = 1e-06
HEAD_FLOOR = 0.01
ARITH_ACCURACY = lax.Precision.HIGHEST

@jax.custom_vjp
def low(v):
    return lax.optimization_barrier(v.astype(jnp.bfloat16)).astype(jnp.float32)

@jax.custom_vjp
def low_back(v):
    return v

def low_keep(v):
    return (low(v), None)

def low_pass(kept, grad):
    return (grad,)

def back_keep(v):
    return (v, None)

def back_low(kept, grad):
    return (low(grad),)
low.defvjp(low_keep, low_pass)
low_back.defvjp(back_keep, back_low)

def matmul(inputs, matrix):
    return jnp.dot(inputs, matrix, precision=ARITH_ACCURACY, preferred_element_type=jnp.float32)

def segment_ids(lengths_row, length):
    bounds = jnp.cumsum(lengths_row).astype(jnp.int32)[:-1]
    position = lax.broadcasted_iota(jnp.int32, (length, bounds.shape[0]), 0)
    return lax.optimization_barrier(jnp.sum((position >= bounds[None, :]).astype(jnp.int32), axis=1)).astype(jnp.int32)

def causal_conv(signal, kernel, segment):
    tap_count = kernel.shape[0]
    length = signal.shape[0]
    padded = jnp.concatenate([jnp.zeros((tap_count - 1, signal.shape[1]), jnp.float32), signal], axis=0)
    seg_pad = jnp.concatenate([jnp.full((tap_count - 1,), -1, jnp.int32), segment])
    summed = kernel[0] * signal
    for offset in range(1, tap_count):
        begin_at = tap_count - 1 - offset
        keep_mask = (seg_pad[begin_at:begin_at + length] == segment).astype(jnp.float32)
        summed = summed + kernel[offset] * padded[begin_at:begin_at + length] * keep_mask[:, None]
    return summed

def span_step(memory_across_tiles, inputs):
    tile_of_probes, key_block, v_block, g_block, b_block, seg_block, seg_before = inputs
    block_width = seg_block.shape[0]
    running_total = jnp.cumsum(g_block, axis=-1)
    row_ids = lax.broadcasted_iota(jnp.int32, (block_width, block_width), 0)
    col_ids = lax.broadcasted_iota(jnp.int32, (block_width, block_width), 1)
    same_seg = seg_block[:, None] == seg_block[None, :]
    upto_mask = same_seg & (row_ids >= col_ids)
    below_mask = same_seg & (row_ids > col_ids)
    continue_state = (seg_block == seg_before).astype(jnp.float32)
    tail_mask = seg_block == seg_block[block_width - 1]
    spread = running_total[:, :, None] - running_total[:, None, :]
    decay_mat = jnp.where(upto_mask, jnp.exp(jnp.where(upto_mask, spread, 0.0)), 0.0)
    key_gram = jnp.einsum('hid,hjd->hij', key_block, key_block, precision=ARITH_ACCURACY)
    lower_mat = jnp.where(below_mask, b_block[:, :, None] * key_gram * decay_mat, 0.0)
    identity = jnp.eye(block_width, dtype=jnp.float32)
    nilpotent = -lower_mat
    inverse = identity + nilpotent
    powered = nilpotent
    for _ in range(block_width.bit_length() - 2):
        powered = jnp.einsum('hij,hjk->hik', powered, powered, precision=ARITH_ACCURACY)
        inverse = inverse + jnp.einsum('hij,hjk->hik', inverse, powered, precision=ARITH_ACCURACY)
    expansion_ratio = jnp.exp(running_total) * continue_state
    corrected_content = jnp.einsum('hij,hjv->hiv', inverse, b_block[:, :, None] * v_block, precision=ARITH_ACCURACY)
    linear_coefficients = jnp.einsum('hij,hjk->hik', inverse, (b_block * expansion_ratio)[:, :, None] * key_block, precision=ARITH_ACCURACY)
    content_corrections = corrected_content - jnp.einsum('vdk,vkz->vdz', linear_coefficients, memory_across_tiles, precision=ARITH_ACCURACY)
    scores = jnp.einsum('hid,hjd->hij', tile_of_probes, key_block, precision=ARITH_ACCURACY) * decay_mat
    tile_result_rows = jnp.einsum('vdk,vkz->vdz', tile_of_probes * expansion_ratio[:, :, None], memory_across_tiles, precision=ARITH_ACCURACY)
    tile_result_rows = tile_result_rows + jnp.einsum('hij,hjv->hiv', scores, content_corrections, precision=ARITH_ACCURACY)
    decay_factor = jnp.where(tail_mask, jnp.exp(jnp.where(tail_mask, running_total[:, block_width - 1:] - running_total, 0.0)), 0.0)
    memory_across_tiles = (jnp.exp(running_total[:, block_width - 1]) * continue_state[block_width - 1])[:, None, None] * memory_across_tiles + jnp.einsum('oln,olm->onm', key_block * decay_factor[:, :, None], content_corrections, precision=ARITH_ACCURACY)
    return (memory_across_tiles, tile_result_rows)

def delta_rule(queries, key_act, values, logdecay, beta_gate, segment):
    length = segment.shape[0]
    block_count = length // SPAN

    def blocks(tensor):
        shaped = tensor.reshape((block_count, SPAN) + tensor.shape[1:])
        return jnp.swapaxes(shaped, 1, 2)
    seg_blocks = segment.reshape(block_count, SPAN)
    seg_before = jnp.concatenate([jnp.full((1,), -1, jnp.int32), seg_blocks[:-1, SPAN - 1]])
    initial = jnp.zeros((queries.shape[1], queries.shape[2], values.shape[2]), jnp.float32)
    final_state, outputs = lax.scan(jax.checkpoint(span_step), initial, (blocks(queries), blocks(key_act), blocks(values), blocks(logdecay), blocks(beta_gate), seg_blocks, seg_before))
    return jnp.swapaxes(outputs, 1, 2).reshape(length, queries.shape[1], values.shape[2])

def mixer(query_in, key_in, value_in, gate_in, decay_in, beta_in, conv_q, conv_k, conv_v, log_rate, rate_bias, head_gain, segment):
    length = segment.shape[0]
    n_heads = decay_in.shape[1]
    queries = jax.nn.silu(causal_conv(query_in, conv_q, segment)).reshape(length, n_heads, -1)
    key_act = jax.nn.silu(causal_conv(key_in, conv_k, segment)).reshape(length, n_heads, -1)
    values = jax.nn.silu(causal_conv(value_in, conv_v, segment)).reshape(length, n_heads, -1)
    queries = queries * lax.rsqrt(lax.optimization_barrier(jnp.sum(queries * queries, axis=-1, keepdims=True)) + EPS)
    key_act = key_act * lax.rsqrt(lax.optimization_barrier(jnp.sum(key_act * key_act, axis=-1, keepdims=True)) + EPS)
    beta_gate = jax.nn.sigmoid(beta_in)
    logdecay = -jnp.exp(log_rate) * jax.nn.softplus(decay_in + rate_bias)
    mixed = delta_rule(queries, key_act, values, logdecay, beta_gate, segment)
    normed = mixed * lax.rsqrt(lax.optimization_barrier(jnp.mean(mixed * mixed, axis=-1, keepdims=True)) + HEAD_FLOOR)
    gated = normed * head_gain * jax.nn.silu(gate_in.reshape(length, n_heads, -1))
    return gated.reshape(length, -1)

def reference(residual, cotangent, lengths, token_order, norm_mixer, w_query, w_key, w_value, w_outgate, w_decay, w_beta, conv_query, conv_key, conv_value, decay_log, decay_bias, norm_head, w_output, norm_ffn, w_gate, w_up, w_down):

    def group_segments(lengths_row):
        return segment_ids(lengths_row, GROUP)
    seg_all = jax.vmap(group_segments)(lengths)

    def layer(res_in, n_mix, m_query, m_key, m_value, m_outgate, m_decay, m_beta, k_query, k_key, k_value, d_log, d_bias, n_head, m_output, n_ffn, m_gate, m_up, m_down):

        def group_fn(pieces):
            source, segment, order_row = pieces
            scale1 = lax.rsqrt(lax.optimization_barrier(jnp.mean(source * source, axis=-1, keepdims=True)) + EPS)
            normed1 = low(source * scale1 * n_mix)

            def project(matrix):
                return low_back(low(matmul(normed1, matrix)))
            q_raw = project(m_query)
            k_raw = project(m_key)
            v_raw = project(m_value)
            g_raw = project(m_outgate)
            d_raw = project(m_decay)
            b_raw = project(m_beta)
            inverse = jnp.zeros_like(order_row).at[order_row].set(lax.iota(jnp.int32, GROUP))
            headout = mixer(q_raw[order_row], k_raw[order_row], v_raw[order_row], g_raw[order_row], d_raw[order_row], b_raw[order_row], k_query, k_key, k_value, d_log, d_bias, n_head, segment)
            given = low_back(low(headout[inverse]))
            attention = low_back(matmul(given, m_output))
            middle = source + attention
            scale2 = lax.rsqrt(lax.optimization_barrier(jnp.mean(middle * middle, axis=-1, keepdims=True)) + EPS)
            normed2 = low(middle * scale2 * n_ffn)
            gating = low_back(matmul(normed2, m_gate))
            up_part = low_back(matmul(normed2, m_up))
            activation = low(jax.nn.silu(gating) * up_part)
            return middle + matmul(activation, m_down)
        groups = res_in.reshape(-1, GROUP, res_in.shape[1])
        stacked = lax.map(jax.checkpoint(group_fn), (groups, seg_all, token_order))
        return stacked.reshape(res_in.shape)
    primals = tuple((param_in.astype(jnp.float32) for param_in in (residual, norm_mixer, w_query, w_key, w_value, w_outgate, w_decay, w_beta, conv_query, conv_key, conv_value, decay_log, decay_bias, norm_head, w_output, norm_ffn, w_gate, w_up, w_down)))
    tile_result_rows, pull_back = jax.vjp(layer, *primals)
    grads = pull_back(cotangent.astype(jnp.float32))
    return (tile_result_rows.astype(jnp.bfloat16), grads[0].astype(jnp.bfloat16), grads[1], grads[2], grads[3], grads[4], grads[5], grads[6], grads[7], grads[8], grads[9], grads[10], grads[11], grads[12], grads[13], grads[14], grads[15], grads[16], grads[17], grads[18])
```

```python
import functools
import jax
import jax.numpy as jnp
from jax import lax
from jax.experimental import pallas as pl
from jax.experimental.pallas import tpu as pltpu
from jax.sharding import PartitionSpec as P

EPS = 1e-06
HEAD_FLOOR = 0.01
SPAN = 128
ROWS = 256
HALO = 16
TAPS = 4
LANES = 128
F32 = jnp.float32
BF16 = jnp.bfloat16
HIGHEST = lax.Precision.HIGHEST


def mm(a, b):
    return lax.dot_general(a.astype(BF16), b.astype(BF16), (((1,), (0,)), ((), ())), preferred_element_type=F32)


def mm_bt(a, b):
    return lax.dot_general(a.astype(BF16), b.astype(BF16), (((1,), (1,)), ((), ())), preferred_element_type=F32)


def mm_at(a, b):
    return lax.dot_general(a.astype(BF16), b.astype(BF16), (((0,), (0,)), ((), ())), preferred_element_type=F32)


def exact(a, b):
    return jnp.dot(a, b, precision=HIGHEST, preferred_element_type=F32)


def iota(shape, axis):
    return lax.broadcasted_iota(jnp.int32, shape, axis)


def bounds_of(lengths):
    found, total = [], 0
    for s in range(lengths.shape[1] - 1):
        total = total + lengths[0, s]
        found.append(total)
    return found


def begin_of(rows, bounds):
    begin = jnp.zeros_like(rows)
    for edge in bounds:
        begin = jnp.where(rows >= edge, edge, begin)
    return begin


def lane_sum(value):
    return jnp.sum(value, axis=1, keepdims=True)


def at_lane(lane, place, column):
    return jnp.where(lane == place, column, 0.0)


def invert(lower):
    size = lower.shape[0]
    row, col = iota((size, size), 0), iota((size, size), 1)
    inverse = jnp.where(row == col, 1.0, jnp.where(row // 2 == col // 2, -lower, 0.0))
    width = 2
    while width < size:
        joint = (row // (2 * width) == col // (2 * width)) & (row // width != col // width)
        between = jnp.where(joint, lower, 0.0)
        held = inverse.astype(BF16)
        inverse = inverse - mm(mm(held, between), held)
        width *= 2
    return inverse


def conv_rows(before, block, taps, pos):
    ext = jnp.concatenate([before, block], axis=0)
    size = block.shape[0]
    total = taps[0:1] * block
    for o in range(1, TAPS):
        total = total + jnp.where(pos >= o, taps[o : o + 1], 0.0) * ext[HALO - o : HALO - o + size]
    return total


def prepare_kernel(heads, key, val, lengths, raw_ref, before_ref, taps_ref, rate_ref,
                   u_ref, qe_ref, w_ref, kd_ref, fresh_ref, p_ref, t_ref, decay_ref, gram_ref, cols_ref):
    wide = heads * (2 * key + val)
    rows = raw_ref.shape[0]
    first = pl.program_id(0) * rows
    bounds = bounds_of(lengths)
    where_row = first + iota((rows, 1), 0)
    begin = begin_of(where_row, bounds)
    pos = where_row - begin
    u = conv_rows(before_ref[:, :wide].astype(F32), raw_ref[:, :wide].astype(F32), taps_ref[...], pos)
    u_ref[...] = u
    act = u / (1.0 + jnp.exp(-u))
    small = raw_ref[:, wide:].astype(F32)
    lane = iota((SPAN, LANES), 1)
    row_i, col_i = iota((SPAN, SPAN), 0), iota((SPAN, SPAN), 1)
    tri = (row_i >= col_i).astype(F32)
    for c in range(rows // SPAN):
        at = slice(c * SPAN, (c + 1) * SPAN)
        base = first + c * SPAN
        begin_c = begin[at]
        begin_r = begin_of(base + iota((1, SPAN), 1), bounds)
        last_begin = begin_of(base + SPAN - 1 + iota((1, 1), 0), bounds)
        shifted = small[at] + rate_ref[1:2]
        soft = jnp.maximum(shifted, 0.0) + jnp.log(1.0 + jnp.exp(-jnp.abs(shifted)))
        slope = 1.0 / (1.0 + jnp.exp(-shifted))
        logd = jnp.where(lane < heads, -jnp.exp(rate_ref[0:1]) * soft, 0.0)
        beta = 1.0 / (1.0 + jnp.exp(-small[at]))
        total = exact(tri, logd)
        total_t = jnp.transpose(total)
        last = total[SPAN - 1 : SPAN]
        reach = jnp.where(begin_c < base, jnp.exp(total), 0.0)
        tail = jnp.where(begin_c == last_begin, jnp.exp(jnp.where(begin_c == last_begin, last - total, 0.0)), 0.0)
        keep = jnp.where(last_begin < base, jnp.exp(last), 0.0)
        two = heads
        cols_ref[at] = (
            jnp.where(lane < two, reach, 0.0)
            + jnp.where((lane >= two) & (lane < 2 * two), beta, 0.0)
            + pltpu.roll(jnp.where(lane < two, tail, 0.0), 2 * two, 1)
            + pltpu.roll(logd, 3 * two, 1)
            + pltpu.roll(jnp.where(lane < two, keep, 0.0), 4 * two, 1)
            + pltpu.roll(jnp.where(lane < two, slope, 0.0), 5 * two, 1)
        )
        same = begin_c == begin_r
        upto = same & (row_i >= col_i)
        for h in range(heads):
            q = act[at, h * key : (h + 1) * key]
            k = act[at, (heads + h) * key : (heads + h + 1) * key]
            v = act[at, 2 * heads * key + h * val : 2 * heads * key + (h + 1) * val]
            q = q * lax.rsqrt(lane_sum(q * q) + EPS)
            k = k * lax.rsqrt(lane_sum(k * k) + EPS)
            b = beta[:, heads + h : heads + h + 1]
            r = reach[:, h : h + 1]
            spread = total[:, h : h + 1] - total_t[h : h + 1]
            decay = jnp.where(upto, jnp.exp(jnp.where(upto, spread, 0.0)), 0.0)
            both = mm_bt(jnp.concatenate([q, k], axis=0), k)
            gram = jnp.where(row_i > col_i, both[SPAN:] * decay, 0.0)
            inverse = invert(b * gram).astype(BF16)
            kat = slice(h * key, (h + 1) * key)
            cat = slice(h * SPAN, (h + 1) * SPAN)
            vat = slice(h * val, (h + 1) * val)
            solved = mm(inverse, jnp.concatenate([b * v, (b * r) * k], axis=1))
            fresh_ref[at, vat] = solved[:, :val]
            w_ref[at, kat] = solved[:, val:].astype(BF16)
            qe_ref[at, kat] = (r * q).astype(BF16)
            kd_ref[at, kat] = (tail[:, h : h + 1] * k).astype(BF16)
            p_ref[at, cat] = both[:SPAN] * decay
            t_ref[at, cat] = inverse
            decay_ref[at, cat] = decay
            gram_ref[at, cat] = gram


def forward_kernel(heads, key, val, qe_ref, w_ref, kd_ref, fresh_ref, p_ref, cols_ref, gate_ref, gain_ref,
                   out_ref, mixed_ref, new_ref, enter_ref, state):
    @pl.when(pl.program_id(0) == 0)
    def _():
        state[...] = jnp.zeros_like(state)

    for h in range(heads):
        kat = slice(h * key, (h + 1) * key)
        cat = slice(h * SPAN, (h + 1) * SPAN)
        vat = slice(h * val, (h + 1) * val)
        carried = state[h]
        low = carried.astype(BF16)
        enter_ref[0, h] = low
        through = mm(jnp.concatenate([w_ref[:, kat], qe_ref[:, kat]], axis=0), low)
        new = (fresh_ref[:, vat] - through[:SPAN]).astype(BF16)
        new_ref[:, vat] = new
        keep = cols_ref[0:1, 4 * heads + h : 4 * heads + h + 1]
        state[h] = keep * carried + mm_at(kd_ref[:, kat], new)
        mixed = through[SPAN:] + mm(p_ref[:, cat], new)
        mixed_ref[:, vat] = mixed
        gate = gate_ref[:, vat].astype(F32)
        scale = lax.rsqrt(lane_sum(mixed * mixed) * (1.0 / val) + HEAD_FLOOR)
        out_ref[:, vat] = (mixed * scale * gain_ref[...] * (gate / (1.0 + jnp.exp(-gate)))).astype(BF16)


def backward_kernel(heads, key, val, grad_ref, mixed_ref, gate_ref, gain_ref, p_ref, qe_ref, w_ref, kd_ref, cols_ref,
                    ggate_ref, gain_out_ref, do_ref, dn_ref, leave_ref, state):
    @pl.when(pl.program_id(0) == 0)
    def _():
        state[...] = jnp.zeros_like(state)
        gain_out_ref[...] = jnp.zeros_like(gain_out_ref)

    for h in range(heads):
        kat = slice(h * key, (h + 1) * key)
        cat = slice(h * SPAN, (h + 1) * SPAN)
        vat = slice(h * val, (h + 1) * val)
        grad = grad_ref[:, vat].astype(F32)
        mixed = mixed_ref[:, vat]
        gate = gate_ref[:, vat].astype(F32)
        gain = gain_ref[...]
        scale = lax.rsqrt(lane_sum(mixed * mixed) * (1.0 / val) + HEAD_FLOOR)
        sig = 1.0 / (1.0 + jnp.exp(-gate))
        silu = gate * sig
        normed = mixed * scale
        ggate_ref[:, vat] = (grad * normed * gain * (sig + silu * (1.0 - sig))).astype(BF16)
        gs = grad * silu
        gain_out_ref[...] += jnp.sum(gs * normed, axis=0, keepdims=True)
        weighted = gs * gain
        do = scale * (weighted - normed * (lane_sum(weighted * normed) * (1.0 / val)))
        do = do.astype(BF16)
        do_ref[:, vat] = do
        carried = state[h]
        low = carried.astype(BF16)
        leave_ref[0, h] = low
        dn = (mm_at(p_ref[:, cat], do) + mm(kd_ref[:, kat], low)).astype(BF16)
        dn_ref[:, vat] = dn
        keep = cols_ref[0:1, 4 * heads + h : 4 * heads + h + 1]
        state[h] = keep * carried + mm_at(
            jnp.concatenate([qe_ref[:, kat], -w_ref[:, kat]], axis=0), jnp.concatenate([do, dn], axis=0)
        )


def finish_kernel(heads, key, val, lengths, raw_ref, before_ref, taps_ref, rate_ref, u_ref, p_ref, t_ref, decay_ref, gram_ref,
                  cols_ref, new_ref, do_ref, dn_ref, enter_ref, leave_ref, dx_ref, gtaps_ref, gsmall_ref, du_ref):
    wide = heads * (2 * key + val)
    rows = raw_ref.shape[0]
    block = pl.num_programs(0) - 1 - pl.program_id(0)
    first = block * rows
    bounds = bounds_of(lengths)

    @pl.when(pl.program_id(0) == 0)
    def _():
        du_ref[rows:] = jnp.zeros((HALO, wide), F32)
        gtaps_ref[...] = jnp.zeros_like(gtaps_ref)
        gsmall_ref[...] = jnp.zeros_like(gsmall_ref)

    @pl.when(pl.program_id(0) > 0)
    def _():
        du_ref[rows:] = du_ref[:HALO]

    lane = iota((SPAN, LANES), 1)
    row_i, col_i = iota((SPAN, SPAN), 0), iota((SPAN, SPAN), 1)
    tri_up = (row_i <= col_i).astype(F32)
    row_c = iota((SPAN, 1), 0)

    def unit(u):
        sig = 1.0 / (1.0 + jnp.exp(-u))
        act = u * sig
        inv = lax.rsqrt(lane_sum(act * act) + EPS)
        return act * inv, inv, sig * (1.0 + u * (1.0 - sig))

    for c in range(rows // SPAN):
        at = slice(c * SPAN, (c + 1) * SPAN)
        cols = cols_ref[at]
        gtotal = jnp.zeros((SPAN, LANES), F32)
        gcross = jnp.zeros((SPAN, SPAN), F32)
        gbeta = jnp.zeros((SPAN, LANES), F32)
        for h in range(heads):
            qat = slice(h * key, (h + 1) * key)
            kat = slice((heads + h) * key, (heads + h + 1) * key)
            xat = slice(2 * heads * key + h * val, 2 * heads * key + (h + 1) * val)
            cat = slice(h * SPAN, (h + 1) * SPAN)
            vat = slice(h * val, (h + 1) * val)
            reach = cols[:, h : h + 1]
            beta = cols[:, heads + h : heads + h + 1]
            tail = cols[:, 2 * heads + h : 2 * heads + h + 1]
            keep = cols[0:1, 4 * heads + h : 4 * heads + h + 1]
            q, q_inv, q_slope = unit(u_ref[at, qat])
            k, k_inv, k_slope = unit(u_ref[at, kat])
            qb, kb = q.astype(BF16), k.astype(BF16)
            new, do = new_ref[at, vat], do_ref[at, vat]
            enter, leave = enter_ref[c, h], leave_ref[c, h]
            decay, gram = decay_ref[at, cat], gram_ref[at, cat]
            dr = mm_at(t_ref[at, cat], dn_ref[at, vat])
            stacked = jnp.concatenate([do, dr.astype(BF16)], axis=0)
            on_new = mm_bt(stacked, new)
            on_state = mm_bt(stacked, enter)
            dp, dl = on_new[:SPAN], -on_new[SPAN:]
            dqe, drs = on_state[:SPAN], on_state[SPAN:]
            dkd = mm_bt(new, leave)
            dpd = (dp * decay).astype(BF16)
            dkk = jnp.where(row_i > col_i, dl * (beta * decay), 0.0)
            dlg = dl * gram
            change = dp * p_ref[at, cat] + beta * dlg
            dq = reach * dqe + mm(dpd, kb)
            dk = (
                tail * dkd
                - (beta * reach) * drs
                + mm(dkk + jnp.transpose(dkk), kb)
                + mm_at(dpd, qb)
            )
            u_v = u_ref[at, xat]
            v_sig = 1.0 / (1.0 + jnp.exp(-u_v))
            v = u_v * v_sig
            drs_k = lane_sum(drs * k)
            dtail = lane_sum(dkd * k) * tail
            gb = lane_sum(dr * v) - reach * drs_k + lane_sum(dlg)
            dlast = jnp.sum(dtail, axis=0, keepdims=True) + keep * jnp.sum(
                lane_sum(enter.astype(F32) * leave.astype(F32)), axis=0, keepdims=True
            )
            gt = lane_sum(change) + reach * (lane_sum(dqe * q) - beta * drs_k) - dtail
            gt = gt + jnp.where(row_c == SPAN - 1, dlast, 0.0)
            gtotal = gtotal + at_lane(lane, h, gt)
            gcross = gcross + jnp.where(row_i == h, jnp.sum(change, axis=0, keepdims=True), 0.0)
            gbeta = gbeta + at_lane(lane, heads + h, gb * beta * (1.0 - beta))
            du_ref[at, qat] = q_inv * (dq - q * lane_sum(dq * q)) * q_slope
            du_ref[at, kat] = k_inv * (dk - k * lane_sum(dk * k)) * k_slope
            du_ref[at, xat] = (beta * dr) * (v_sig * (1.0 + u_v * (1.0 - v_sig)))
        glog = exact(tri_up, gtotal - jnp.transpose(gcross))
        logd = jnp.where(lane < heads, pltpu.roll(cols, LANES - 3 * heads, 1), 0.0)
        slope = jnp.where(lane < heads, pltpu.roll(cols, LANES - 5 * heads, 1), 0.0)
        gdecay = -glog * jnp.exp(rate_ref[0:1]) * slope
        gsmall_ref[0:1] += jnp.sum(glog * logd, axis=0, keepdims=True)
        gsmall_ref[1:2] += jnp.sum(gdecay, axis=0, keepdims=True)
        dx_ref[at, wide:] = (gdecay + gbeta).astype(BF16)
    where_row = first + iota((rows, 1), 0)
    pos = where_row - begin_of(where_row, bounds)
    ext = jnp.concatenate([before_ref[:, :wide].astype(F32), raw_ref[:, :wide].astype(F32)], axis=0)
    du = du_ref[:rows]
    dx = taps_ref[0:1] * du
    gtaps_ref[0:1] += jnp.sum(du * ext[HALO:], axis=0, keepdims=True)
    for o in range(1, TAPS):
        ahead = where_row + o
        pos_ahead = ahead - begin_of(ahead, bounds)
        dx = dx + jnp.where(pos_ahead >= o, taps_ref[o : o + 1], 0.0) * du_ref[o : o + rows]
        gtaps_ref[o : o + 1] += jnp.sum(
            jnp.where(pos >= o, du, 0.0) * ext[HALO - o : HALO - o + rows], axis=0, keepdims=True
        )
    dx_ref[:, :wide] = dx.astype(BF16)


def cost(flops, moved):
    return pl.CostEstimate(flops=int(flops), bytes_accessed=int(moved), transcendentals=0)


def params():
    return pltpu.CompilerParams(dimension_semantics=("arbitrary",), vmem_limit_bytes=56 * 2**20)


def prepare(raw, taps, rates, lengths, heads, key, val):
    length, width = raw.shape
    wide = heads * (2 * key + val)
    steps = length // ROWS
    ratio = ROWS // HALO
    row = lambda w: pl.BlockSpec((ROWS, w), lambda i: (i, 0))
    whole = lambda a: pl.BlockSpec(a.shape, lambda i: (0, 0))
    shape = lambda w, t: jax.ShapeDtypeStruct((length, w), t)
    kinds = [(wide, F32), (heads * key, BF16), (heads * key, BF16), (heads * key, BF16), (heads * val, F32),
             (heads * SPAN, F32), (heads * SPAN, BF16), (heads * SPAN, F32), (heads * SPAN, F32), (LANES, F32)]
    return pl.pallas_call(
        functools.partial(prepare_kernel, heads, key, val),
        grid=(steps,),
        in_specs=[
            pl.BlockSpec(memory_space=pltpu.SMEM),
            row(width),
            pl.BlockSpec((HALO, width), lambda i: (jnp.maximum(i * ratio - 1, 0), 0)),
            whole(taps),
            whole(rates),
        ],
        out_specs=[row(w) for w, _ in kinds],
        out_shape=[shape(w, t) for w, t in kinds],
        compiler_params=params(),
        cost_estimate=cost(40e9, 40e6),
        name="prepare",
    )(lengths, raw, raw, taps, rates)


def forward(qe, w, kd, fresh, p, cols, gate, gain, heads, key, val):
    length = qe.shape[0]
    steps = length // SPAN
    row = lambda a: pl.BlockSpec((SPAN, a.shape[1]), lambda i: (i, 0))
    given = [qe, w, kd, fresh, p, cols, gate]
    wide = heads * val
    kinds = [(wide, BF16), (wide, F32), (wide, BF16)]
    return pl.pallas_call(
        functools.partial(forward_kernel, heads, key, val),
        grid=(steps,),
        in_specs=[row(a) for a in given] + [pl.BlockSpec(gain.shape, lambda i: (0, 0))],
        out_specs=[pl.BlockSpec((SPAN, wd), lambda i: (i, 0)) for wd, _ in kinds]
        + [pl.BlockSpec((1, heads, key, val), lambda i: (i, 0, 0, 0))],
        out_shape=[jax.ShapeDtypeStruct((length, wd), t) for wd, t in kinds]
        + [jax.ShapeDtypeStruct((steps, heads, key, val), BF16)],
        scratch_shapes=[pltpu.VMEM((heads, key, val), F32)],
        compiler_params=params(),
        cost_estimate=cost(20e9, 20e6),
        name="forward",
    )(*given, gain)


def backward(grad, mixed, gate, gain, p, qe, w, kd, cols, heads, key, val):
    length = qe.shape[0]
    steps = length // SPAN
    row = lambda a: pl.BlockSpec((SPAN, a.shape[1]), lambda i: (steps - 1 - i, 0))
    wide = heads * val
    kinds = [wide, wide, wide]
    back = pl.BlockSpec((SPAN, wide), lambda i: (steps - 1 - i, 0))
    full = jax.ShapeDtypeStruct((length, wide), BF16)
    return pl.pallas_call(
        functools.partial(backward_kernel, heads, key, val),
        grid=(steps,),
        in_specs=[row(grad), row(mixed), row(gate), pl.BlockSpec(gain.shape, lambda i: (0, 0)), row(p), row(qe), row(w),
                  row(kd), row(cols)],
        out_specs=[back, pl.BlockSpec((1, val), lambda i: (0, 0)), back, back,
                   pl.BlockSpec((1, heads, key, val), lambda i: (steps - 1 - i, 0, 0, 0))],
        out_shape=[full, jax.ShapeDtypeStruct((1, val), F32), full, full,
                   jax.ShapeDtypeStruct((steps, heads, key, val), BF16)],
        scratch_shapes=[pltpu.VMEM((heads, key, val), F32)],
        compiler_params=params(),
        cost_estimate=cost(25e9, 25e6),
        name="backward",
    )(grad, mixed, gate, gain, p, qe, w, kd, cols)


def finish(raw, taps, rates, lengths, u, p, t, decay, gram, cols, new, do, dn, enter, leave, heads, key, val):
    length, width = raw.shape
    wide = heads * (2 * key + val)
    steps = length // ROWS
    ratio = ROWS // HALO
    per = ROWS // SPAN
    row = lambda a: pl.BlockSpec((ROWS, a.shape[1]), lambda i: (steps - 1 - i, 0))
    states = pl.BlockSpec((per, heads, key, val), lambda i: (steps - 1 - i, 0, 0, 0))
    whole = lambda a: pl.BlockSpec(a.shape, lambda i: (0, 0))
    fixed = lambda s: pl.BlockSpec(s, lambda i: (0, 0))
    given = [u, p, t, decay, gram, cols, new, do, dn]
    return pl.pallas_call(
        functools.partial(finish_kernel, heads, key, val),
        grid=(steps,),
        in_specs=[
            pl.BlockSpec(memory_space=pltpu.SMEM),
            row(raw),
            pl.BlockSpec((HALO, width), lambda i: (jnp.maximum((steps - 1 - i) * ratio - 1, 0), 0)),
            whole(taps),
            whole(rates),
        ] + [row(a) for a in given] + [states, states],
        out_specs=[row(raw), fixed((8, wide)), fixed((8, LANES))],
        out_shape=[jax.ShapeDtypeStruct((length, width), BF16), jax.ShapeDtypeStruct((8, wide), F32),
                   jax.ShapeDtypeStruct((8, LANES), F32)],
        scratch_shapes=[pltpu.VMEM((ROWS + HALO, wide), F32)],
        compiler_params=params(),
        cost_estimate=cost(60e9, 50e6),
        name="finish",
    )(lengths, raw, raw, taps, rates, *given, enter, leave)


def dense(a, b):
    return jnp.dot(a, b, preferred_element_type=F32)


def dense_t(a, b):
    return lax.dot_general(a, b, (((0,), (0,)), ((), ())), preferred_element_type=F32)


def dense_bt(a, b):
    return lax.dot_general(a, b, (((1,), (1,)), ((), ())), preferred_element_type=F32)


def local(
    residual, cotangent, lengths, token_order, norm_mixer, w_query, w_key, w_value, w_outgate, w_decay, w_beta,
    conv_query, conv_key, conv_value, decay_log, decay_bias, norm_head, w_output, norm_ffn, w_gate, w_up, w_down,
):
    n_ctx, n_tp = lax.axis_size("ctx"), lax.axis_size("tp")
    at_ctx, at_tp = lax.axis_index("ctx"), lax.axis_index("tp")
    rows_d = w_query.shape[0]
    heads = w_decay.shape[1] // n_ctx
    key = w_query.shape[1] // (n_ctx * heads)
    val = w_value.shape[1] // (n_ctx * heads)
    hk, hv = heads * key, heads * val
    wide = 2 * hk + hv
    units = w_gate.shape[1] // n_ctx
    group = token_order.shape[1]
    mine = group // (n_ctx * n_tp)

    def cut(w):
        return w.reshape(rows_d, n_ctx, w.shape[1] // n_ctx)

    def spread(*parts):
        block = jnp.swapaxes(jnp.concatenate(parts, axis=2), 0, 1)
        block = lax.all_to_all(block, "ctx", split_axis=0, concat_axis=0, tiled=True)
        return lax.all_gather(block.reshape(n_ctx * rows_d, -1), "fsdp", axis=0, tiled=True)

    def own(partial):
        block = lax.psum_scatter(partial.astype(BF16), "fsdp", scatter_dimension=0, tiled=True)
        block = block.reshape(n_ctx, rows_d, -1)
        block = lax.all_to_all(block, "ctx", split_axis=0, concat_axis=0, tiled=True)
        return jnp.swapaxes(block, 0, 1).astype(F32)

    def join(block, begin, end):
        return block[:, :, begin:end].reshape(rows_d, -1)

    gains = jnp.stack([norm_mixer, norm_ffn], axis=1)[:, None, :]
    gains = jnp.broadcast_to(gains, (rows_d, n_ctx, 2))
    blank = jnp.zeros((rows_d, n_ctx, LANES - 2 * heads - 2), BF16)
    w_first = spread(cut(w_query), cut(w_key), cut(w_value), cut(w_decay), cut(w_beta), gains, blank)
    w_second = spread(cut(w_outgate), cut(w_output.T))
    w_hidden = spread(cut(w_gate), cut(w_up))
    w_last = spread(cut(w_down.T))
    w_gates, w_out = w_second[:, :hv], w_second[:, hv:]
    n_mix = w_first[:, wide + 2 * heads].astype(F32)
    n_ffn = w_first[:, wide + 2 * heads + 1].astype(F32)

    order = token_order[0]
    inverse = jnp.zeros_like(order).at[order].set(lax.iota(jnp.int32, group))
    tokens = lax.all_gather(residual, "ctx", axis=0, tiled=True)
    packed = tokens[order].astype(F32)
    scale = lax.rsqrt(jnp.mean(packed * packed, axis=-1, keepdims=True) + EPS)
    normed1 = (packed * scale * n_mix).astype(BF16)
    raw = dense(normed1, w_first).astype(BF16)
    gate = dense(normed1, w_gates).astype(BF16)

    first_head = (at_tp * n_ctx + at_ctx) * heads

    def share(conv, width):
        return lax.dynamic_slice_in_dim(conv.astype(F32), first_head * width, heads * width, 1)

    taps = jnp.concatenate([share(conv_query, key), share(conv_key, key), share(conv_value, val)], axis=1)
    taps = jnp.concatenate([taps, jnp.zeros_like(taps)], axis=0)
    rates = jnp.stack([
        lax.dynamic_slice_in_dim(decay_log, first_head, heads, 0),
        lax.dynamic_slice_in_dim(decay_bias, first_head, heads, 0),
    ])
    rates = jnp.pad(rates, ((0, 6), (0, LANES - heads)))
    gain = norm_head.astype(F32)[None, :]
    sizes = (heads, key, val)
    u, qe, wm, kd, fresh, p, solve, decay, gram, cols = prepare(raw, taps, rates, lengths, *sizes)
    headout, mixed, new, enter = forward(qe, wm, kd, fresh, p, cols, gate, gain, *sizes)

    both = ("ctx", "tp")
    given = headout[inverse]
    attention = lax.psum_scatter(
        dense_bt(given, w_out).astype(BF16), both, scatter_dimension=0, tiled=True
    ).astype(F32)
    source = lax.dynamic_slice_in_dim(residual, at_tp * mine, mine, 0).astype(F32)
    middle = source + attention
    scale2 = lax.rsqrt(jnp.mean(middle * middle, axis=-1, keepdims=True) + EPS)
    normed2 = (middle * scale2 * n_ffn).astype(BF16)
    normed2 = lax.all_gather(normed2, both, axis=0, tiled=True)
    hidden = dense(normed2, w_hidden)
    gating, up_part = hidden[:, :units], hidden[:, units:]
    sig = jax.nn.sigmoid(gating)
    silu = gating * sig
    activation = (silu * up_part).astype(BF16)

    cot = lax.all_gather(cotangent, "ctx", axis=0, tiled=True)
    grad_act = dense(cot, w_last)
    grad_gating = (grad_act * up_part * (sig + silu * (1.0 - sig))).astype(BF16)
    grad_up = (grad_act * silu).astype(BF16)
    grad_hidden = jnp.concatenate([grad_gating, grad_up], axis=1)
    grad_normed2 = lax.psum_scatter(
        dense_bt(grad_hidden, w_hidden).astype(BF16), both, scatter_dimension=0, tiled=True
    ).astype(F32)

    def norm_back(u_in, s, n, g):
        weighted = n * g
        return s * weighted - u_in * (s * s * s) * jnp.mean(u_in * weighted, axis=-1, keepdims=True)

    cot_mine = lax.dynamic_slice_in_dim(cotangent, at_tp * mine, mine, 0).astype(F32)
    grad_mid = cot_mine + norm_back(middle, scale2, n_ffn, grad_normed2)
    grad_attn = lax.all_gather(grad_mid.astype(BF16), both, axis=0, tiled=True)
    grad_given = dense(grad_attn, w_out).astype(BF16)

    ffn_out = lax.psum_scatter(
        dense_bt(activation, w_last).astype(BF16), both, scatter_dimension=0, tiled=True
    ).astype(F32)
    output = lax.all_gather((middle + ffn_out).astype(BF16), "tp", axis=0, tiled=True)

    grad_gate, g_gain, do, dn, leave = backward(
        grad_given[order], mixed, gate, gain, p, qe, wm, kd, cols, *sizes
    )
    dx, g_taps, g_small = finish(
        raw, taps, rates, lengths, u, p, solve, decay, gram, cols, new, do, dn, enter, leave, *sizes
    )
    grad_packed = jnp.concatenate([dx, grad_gate], axis=1)
    w_all = jnp.concatenate([w_first, w_gates], axis=1)
    grad_normed1 = lax.psum_scatter(
        dense_bt(grad_packed[inverse], w_all).astype(BF16), both, scatter_dimension=0, tiled=True
    ).astype(F32)
    scale1 = lax.rsqrt(jnp.mean(source * source, axis=-1, keepdims=True) + EPS)
    grad_input = (grad_mid + norm_back(source, scale1, n_mix, grad_normed1)).astype(BF16)
    grad_input = lax.all_gather(grad_input, "tp", axis=0, tiled=True)

    g_hidden = own(dense_t(normed2, grad_hidden))
    g_last = own(dense_t(cot, activation))
    g_out = own(dense_t(grad_attn, given))
    g_gates = own(dense_t(normed1, grad_gate))
    g_first = own(dense_t(normed1, dx))

    gw_gate, gw_up = join(g_hidden, 0, units), join(g_hidden, units, 2 * units)
    gw_down = join(g_last, 0, units).T
    gw_output = join(g_out, 0, hv).T
    gw_outgate = join(g_gates, 0, hv)
    gw_query, gw_key = join(g_first, 0, hk), join(g_first, hk, 2 * hk)
    gw_value = join(g_first, 2 * hk, wide)
    gw_decay = join(g_first, wide, wide + heads)
    gw_beta = join(g_first, wide + heads, wide + 2 * heads)

    def overlap(*pairs):
        return sum(jnp.sum(w.astype(F32) * g, axis=1) for w, g in pairs)

    g_norms = jnp.stack([
        overlap((w_query, gw_query), (w_key, gw_key), (w_value, gw_value), (w_outgate, gw_outgate),
                (w_decay, gw_decay), (w_beta, gw_beta)) / norm_mixer.astype(F32),
        overlap((w_gate, gw_gate), (w_up, gw_up)) / norm_ffn.astype(F32),
    ])
    g_norms = lax.psum(g_norms, "tp")

    def place(like, part, width):
        return lax.dynamic_update_slice_in_dim(jnp.zeros(like, F32), part, first_head * width, len(like) - 1)

    sums = lax.psum(
        jnp.concatenate([
            place(conv_query.shape, g_taps[:TAPS, :hk], key).reshape(-1),
            place(conv_key.shape, g_taps[:TAPS, hk : 2 * hk], key).reshape(-1),
            place(conv_value.shape, g_taps[:TAPS, 2 * hk :], val).reshape(-1),
            place(decay_log.shape, g_small[0, :heads], 1),
            place(decay_bias.shape, g_small[1, :heads], 1),
            g_gain[0],
        ]),
        ("fsdp", "ctx", "tp"),
    )
    pieces, at = [], 0
    for like in (conv_query, conv_key, conv_value, decay_log, decay_bias, norm_head):
        pieces.append(sums[at : at + like.size].reshape(like.shape))
        at += like.size
    return (
        output, grad_input, g_norms[0], gw_query, gw_key, gw_value, gw_outgate, gw_decay, gw_beta,
        *pieces, gw_output, g_norms[1], gw_gate, gw_up, gw_down,
    )


def solution(mesh):
    rows = ("fsdp", "ctx")
    up, down, vector, copied = P(rows, "tp"), P("tp", rows), P(rows), P()
    in_specs = (
        P(rows, None), P(rows, None), P("fsdp", None), P("fsdp", None), vector, up, up, up, up, up, up,
        copied, copied, copied, copied, copied, copied, down, vector, up, up, down,
    )
    out_specs = (
        P(rows, None), P(rows, None), vector, up, up, up, up, up, up,
        copied, copied, copied, copied, copied, copied, down, vector, up, up, down,
    )
    return jax.shard_map(local, mesh=mesh, in_specs=in_specs, out_specs=out_specs, check_vma=False)
```

```python
import functools
import jax
import jax.numpy as jnp
from jax import lax
from jax.experimental import pallas as pl
from jax.experimental.pallas import tpu as pltpu
from jax.sharding import PartitionSpec as P

EPS = 1e-06
HEAD_FLOOR = 0.01
SPAN = 128
ROWS = 256
HALO = 16
TAPS = 4
LANES = 128
F32 = jnp.float32
BF16 = jnp.bfloat16
HIGHEST = lax.Precision.HIGHEST


def mm(a, b):
    return lax.dot_general(a.astype(BF16), b.astype(BF16), (((1,), (0,)), ((), ())), preferred_element_type=F32)


def mm_bt(a, b):
    return lax.dot_general(a.astype(BF16), b.astype(BF16), (((1,), (1,)), ((), ())), preferred_element_type=F32)


def mm_at(a, b):
    return lax.dot_general(a.astype(BF16), b.astype(BF16), (((0,), (0,)), ((), ())), preferred_element_type=F32)


def exact(a, b):
    return jnp.dot(a, b, precision=HIGHEST, preferred_element_type=F32)


def iota(shape, axis):
    return lax.broadcasted_iota(jnp.int32, shape, axis)


def bounds_of(lengths):
    found, total = [], 0
    for s in range(lengths.shape[1] - 1):
        total = total + lengths[0, s]
        found.append(total)
    return found


def begin_of(rows, bounds):
    begin = jnp.zeros_like(rows)
    for edge in bounds:
        begin = jnp.where(rows >= edge, edge, begin)
    return begin


def lane_sum(value):
    return jnp.sum(value, axis=1, keepdims=True)


def at_lane(lane, place, column):
    return jnp.where(lane == place, column, 0.0)


def invert(lower):
    size = lower.shape[0]
    row, col = iota((size, size), 0), iota((size, size), 1)
    inverse = jnp.where(row == col, 1.0, jnp.where(row // 2 == col // 2, -lower, 0.0))
    width = 2
    while width < size:
        joint = (row // (2 * width) == col // (2 * width)) & (row // width != col // width)
        between = jnp.where(joint, lower, 0.0)
        held = inverse.astype(BF16)
        inverse = inverse - mm(mm(held, between), held)
        width *= 2
    return inverse


def conv_rows(before, block, taps, pos):
    ext = jnp.concatenate([before, block], axis=0)
    size = block.shape[0]
    total = taps[0:1] * block
    for o in range(1, TAPS):
        total = total + jnp.where(pos >= o, taps[o : o + 1], 0.0) * ext[HALO - o : HALO - o + size]
    return total


def prepare_kernel(heads, key, val, n_wait, lengths, raw_ref, before_ref, small_ref, taps_ref, rate_ref, *refs):
    prepare_block(heads, key, val, lengths, raw_ref, before_ref, small_ref, taps_ref, rate_ref, *refs[n_wait:])


def prepare_block(heads, key, val, lengths, raw_ref, before_ref, small_ref, taps_ref, rate_ref,
                   u_ref, qe_ref, w_ref, kd_ref, fresh_ref, p_ref, t_ref, decay_ref, gram_ref, cols_ref):
    rows = raw_ref.shape[0]
    first = pl.program_id(0) * rows
    bounds = bounds_of(lengths)
    where_row = first + iota((rows, 1), 0)
    begin = begin_of(where_row, bounds)
    pos = where_row - begin
    u = conv_rows(before_ref[...].astype(F32), raw_ref[...].astype(F32), taps_ref[...], pos)
    u_ref[...] = u
    act = u / (1.0 + jnp.exp(-u))
    small = small_ref[...].astype(F32)
    lane = iota((SPAN, LANES), 1)
    row_i, col_i = iota((SPAN, SPAN), 0), iota((SPAN, SPAN), 1)
    tri = (row_i >= col_i).astype(F32)
    for c in range(rows // SPAN):
        at = slice(c * SPAN, (c + 1) * SPAN)
        base = first + c * SPAN
        begin_c = begin[at]
        begin_r = begin_of(base + iota((1, SPAN), 1), bounds)
        last_begin = begin_of(base + SPAN - 1 + iota((1, 1), 0), bounds)
        shifted = small[at] + rate_ref[1:2]
        soft = jnp.maximum(shifted, 0.0) + jnp.log(1.0 + jnp.exp(-jnp.abs(shifted)))
        slope = 1.0 / (1.0 + jnp.exp(-shifted))
        logd = jnp.where(lane < heads, -jnp.exp(rate_ref[0:1]) * soft, 0.0)
        beta = 1.0 / (1.0 + jnp.exp(-small[at]))
        total = exact(tri, logd)
        total_t = jnp.transpose(total)
        last = total[SPAN - 1 : SPAN]
        reach = jnp.where(begin_c < base, jnp.exp(total), 0.0)
        tail = jnp.where(begin_c == last_begin, jnp.exp(jnp.where(begin_c == last_begin, last - total, 0.0)), 0.0)
        keep = jnp.where(last_begin < base, jnp.exp(last), 0.0)
        two = heads
        cols_ref[at] = (
            jnp.where(lane < two, reach, 0.0)
            + jnp.where((lane >= two) & (lane < 2 * two), beta, 0.0)
            + pltpu.roll(jnp.where(lane < two, tail, 0.0), 2 * two, 1)
            + pltpu.roll(logd, 3 * two, 1)
            + pltpu.roll(jnp.where(lane < two, keep, 0.0), 4 * two, 1)
            + pltpu.roll(jnp.where(lane < two, slope, 0.0), 5 * two, 1)
        )
        same = begin_c == begin_r
        upto = same & (row_i >= col_i)
        for h in range(heads):
            q = act[at, h * key : (h + 1) * key]
            k = act[at, (heads + h) * key : (heads + h + 1) * key]
            v = act[at, 2 * heads * key + h * val : 2 * heads * key + (h + 1) * val]
            q = q * lax.rsqrt(lane_sum(q * q) + EPS)
            k = k * lax.rsqrt(lane_sum(k * k) + EPS)
            b = beta[:, heads + h : heads + h + 1]
            r = reach[:, h : h + 1]
            spread = total[:, h : h + 1] - total_t[h : h + 1]
            decay = jnp.where(upto, jnp.exp(jnp.where(upto, spread, 0.0)), 0.0)
            both = mm_bt(jnp.concatenate([q, k], axis=0), k)
            gram = jnp.where(row_i > col_i, both[SPAN:] * decay, 0.0)
            inverse = invert(b * gram).astype(BF16)
            kat = slice(h * key, (h + 1) * key)
            cat = slice(h * SPAN, (h + 1) * SPAN)
            vat = slice(h * val, (h + 1) * val)
            solved = mm(inverse, jnp.concatenate([b * v, (b * r) * k], axis=1))
            fresh_ref[at, vat] = solved[:, :val]
            w_ref[at, kat] = solved[:, val:].astype(BF16)
            qe_ref[at, kat] = (r * q).astype(BF16)
            kd_ref[at, kat] = (tail[:, h : h + 1] * k).astype(BF16)
            p_ref[at, cat] = both[:SPAN] * decay
            t_ref[at, cat] = inverse
            decay_ref[at, cat] = decay
            gram_ref[at, cat] = gram


def forward_kernel(heads, key, val, n_wait, qe_ref, w_ref, kd_ref, fresh_ref, p_ref, cols_ref, normed_ref, gate_w_ref,
                   gain_ref, *refs):
    out_ref, mixed_ref, new_ref, gate_ref, enter_ref, state = refs[n_wait:]

    @pl.when(pl.program_id(0) == 0)
    def _():
        state[...] = jnp.zeros_like(state)

    gates = mm(normed_ref[...], gate_w_ref[...]).astype(BF16)
    gate_ref[...] = gates
    for h in range(heads):
        kat = slice(h * key, (h + 1) * key)
        cat = slice(h * SPAN, (h + 1) * SPAN)
        vat = slice(h * val, (h + 1) * val)
        carried = state[h]
        low = carried.astype(BF16)
        enter_ref[0, h] = low
        through = mm(jnp.concatenate([w_ref[:, kat], qe_ref[:, kat]], axis=0), low)
        new = (fresh_ref[:, vat] - through[:SPAN]).astype(BF16)
        new_ref[:, vat] = new
        keep = cols_ref[0:1, 4 * heads + h : 4 * heads + h + 1]
        state[h] = keep * carried + mm_at(kd_ref[:, kat], new)
        mixed = through[SPAN:] + mm(p_ref[:, cat], new)
        mixed_ref[:, vat] = mixed
        gate = gates[:, vat].astype(F32)
        scale = lax.rsqrt(lane_sum(mixed * mixed) * (1.0 / val) + HEAD_FLOOR)
        out_ref[:, vat] = (mixed * scale * gain_ref[...] * (gate / (1.0 + jnp.exp(-gate)))).astype(BF16)


def backward_kernel(heads, key, val, n_wait, grad_ref, mixed_ref, gate_ref, gain_ref, p_ref, qe_ref, w_ref, kd_ref,
                    cols_ref, *refs):
    ggate_ref, gain_out_ref, do_ref, dn_ref, leave_ref, state = refs[n_wait:]

    @pl.when(pl.program_id(0) == 0)
    def _():
        state[...] = jnp.zeros_like(state)
        gain_out_ref[...] = jnp.zeros_like(gain_out_ref)

    for h in range(heads):
        kat = slice(h * key, (h + 1) * key)
        cat = slice(h * SPAN, (h + 1) * SPAN)
        vat = slice(h * val, (h + 1) * val)
        grad = grad_ref[:, vat].astype(F32)
        mixed = mixed_ref[:, vat]
        gate = gate_ref[:, vat].astype(F32)
        gain = gain_ref[...]
        scale = lax.rsqrt(lane_sum(mixed * mixed) * (1.0 / val) + HEAD_FLOOR)
        sig = 1.0 / (1.0 + jnp.exp(-gate))
        silu = gate * sig
        normed = mixed * scale
        ggate_ref[:, vat] = (grad * normed * gain * (sig + silu * (1.0 - sig))).astype(BF16)
        gs = grad * silu
        gain_out_ref[...] += jnp.sum(gs * normed, axis=0, keepdims=True)
        weighted = gs * gain
        do = scale * (weighted - normed * (lane_sum(weighted * normed) * (1.0 / val)))
        do = do.astype(BF16)
        do_ref[:, vat] = do
        carried = state[h]
        low = carried.astype(BF16)
        leave_ref[0, h] = low
        dn = (mm_at(p_ref[:, cat], do) + mm(kd_ref[:, kat], low)).astype(BF16)
        dn_ref[:, vat] = dn
        keep = cols_ref[0:1, 4 * heads + h : 4 * heads + h + 1]
        state[h] = keep * carried + mm_at(
            jnp.concatenate([qe_ref[:, kat], -w_ref[:, kat]], axis=0), jnp.concatenate([do, dn], axis=0)
        )


def finish_kernel(heads, key, val, n_wait, lengths, raw_ref, before_ref, taps_ref, rate_ref, u_ref, p_ref, t_ref, decay_ref,
                  gram_ref, cols_ref, new_ref, do_ref, dn_ref, ggate_ref, enter_ref, leave_ref, *refs):
    dx_ref, dsmall_ref, all_ref, gtaps_ref, gsmall_ref, du_ref = refs[n_wait:]
    wide = heads * (2 * key + val)
    rows = raw_ref.shape[0]
    block = pl.num_programs(0) - 1 - pl.program_id(0)
    first = block * rows
    bounds = bounds_of(lengths)

    @pl.when(pl.program_id(0) == 0)
    def _():
        du_ref[rows:] = jnp.zeros((HALO, wide), F32)
        gtaps_ref[...] = jnp.zeros_like(gtaps_ref)
        gsmall_ref[...] = jnp.zeros_like(gsmall_ref)

    @pl.when(pl.program_id(0) > 0)
    def _():
        du_ref[rows:] = du_ref[:HALO]

    lane = iota((SPAN, LANES), 1)
    row_i, col_i = iota((SPAN, SPAN), 0), iota((SPAN, SPAN), 1)
    tri_up = (row_i <= col_i).astype(F32)
    row_c = iota((SPAN, 1), 0)

    def unit(u):
        sig = 1.0 / (1.0 + jnp.exp(-u))
        act = u * sig
        inv = lax.rsqrt(lane_sum(act * act) + EPS)
        return act * inv, inv, sig * (1.0 + u * (1.0 - sig))

    for c in range(rows // SPAN):
        at = slice(c * SPAN, (c + 1) * SPAN)
        cols = cols_ref[at]
        gtotal = jnp.zeros((SPAN, LANES), F32)
        gcross = jnp.zeros((SPAN, SPAN), F32)
        gbeta = jnp.zeros((SPAN, LANES), F32)
        for h in range(heads):
            qat = slice(h * key, (h + 1) * key)
            kat = slice((heads + h) * key, (heads + h + 1) * key)
            xat = slice(2 * heads * key + h * val, 2 * heads * key + (h + 1) * val)
            cat = slice(h * SPAN, (h + 1) * SPAN)
            vat = slice(h * val, (h + 1) * val)
            reach = cols[:, h : h + 1]
            beta = cols[:, heads + h : heads + h + 1]
            tail = cols[:, 2 * heads + h : 2 * heads + h + 1]
            keep = cols[0:1, 4 * heads + h : 4 * heads + h + 1]
            q, q_inv, q_slope = unit(u_ref[at, qat])
            k, k_inv, k_slope = unit(u_ref[at, kat])
            qb, kb = q.astype(BF16), k.astype(BF16)
            new, do = new_ref[at, vat], do_ref[at, vat]
            enter, leave = enter_ref[c, h], leave_ref[c, h]
            decay, gram = decay_ref[at, cat], gram_ref[at, cat]
            dr = mm_at(t_ref[at, cat], dn_ref[at, vat])
            stacked = jnp.concatenate([do, dr.astype(BF16)], axis=0)
            on_new = mm_bt(stacked, new)
            on_state = mm_bt(stacked, enter)
            dp, dl = on_new[:SPAN], -on_new[SPAN:]
            dqe, drs = on_state[:SPAN], on_state[SPAN:]
            dkd = mm_bt(new, leave)
            dpd = (dp * decay).astype(BF16)
            dkk = jnp.where(row_i > col_i, dl * (beta * decay), 0.0)
            dlg = dl * gram
            change = dp * p_ref[at, cat] + beta * dlg
            dq = reach * dqe + mm(dpd, kb)
            dk = (
                tail * dkd
                - (beta * reach) * drs
                + mm(dkk + jnp.transpose(dkk), kb)
                + mm_at(dpd, qb)
            )
            u_v = u_ref[at, xat]
            v_sig = 1.0 / (1.0 + jnp.exp(-u_v))
            v = u_v * v_sig
            drs_k = lane_sum(drs * k)
            dtail = lane_sum(dkd * k) * tail
            gb = lane_sum(dr * v) - reach * drs_k + lane_sum(dlg)
            dlast = jnp.sum(dtail, axis=0, keepdims=True) + keep * jnp.sum(
                lane_sum(enter.astype(F32) * leave.astype(F32)), axis=0, keepdims=True
            )
            gt = lane_sum(change) + reach * (lane_sum(dqe * q) - beta * drs_k) - dtail
            gt = gt + jnp.where(row_c == SPAN - 1, dlast, 0.0)
            gtotal = gtotal + at_lane(lane, h, gt)
            gcross = gcross + jnp.where(row_i == h, jnp.sum(change, axis=0, keepdims=True), 0.0)
            gbeta = gbeta + at_lane(lane, heads + h, gb * beta * (1.0 - beta))
            du_ref[at, qat] = q_inv * (dq - q * lane_sum(dq * q)) * q_slope
            du_ref[at, kat] = k_inv * (dk - k * lane_sum(dk * k)) * k_slope
            du_ref[at, xat] = (beta * dr) * (v_sig * (1.0 + u_v * (1.0 - v_sig)))
        glog = exact(tri_up, gtotal - jnp.transpose(gcross))
        logd = jnp.where(lane < heads, pltpu.roll(cols, LANES - 3 * heads, 1), 0.0)
        slope = jnp.where(lane < heads, pltpu.roll(cols, LANES - 5 * heads, 1), 0.0)
        gdecay = -glog * jnp.exp(rate_ref[0:1]) * slope
        gsmall_ref[0:1] += jnp.sum(glog * logd, axis=0, keepdims=True)
        gsmall_ref[1:2] += jnp.sum(gdecay, axis=0, keepdims=True)
        dsmall_ref[at] = (gdecay + gbeta).astype(BF16)
    where_row = first + iota((rows, 1), 0)
    pos = where_row - begin_of(where_row, bounds)
    ext = jnp.concatenate([before_ref[...].astype(F32), raw_ref[...].astype(F32)], axis=0)
    du = du_ref[:rows]
    dx = taps_ref[0:1] * du
    gtaps_ref[0:1] += jnp.sum(du * ext[HALO:], axis=0, keepdims=True)
    for o in range(1, TAPS):
        ahead = where_row + o
        pos_ahead = ahead - begin_of(ahead, bounds)
        dx = dx + jnp.where(pos_ahead >= o, taps_ref[o : o + 1], 0.0) * du_ref[o : o + rows]
        gtaps_ref[o : o + 1] += jnp.sum(
            jnp.where(pos >= o, du, 0.0) * ext[HALO - o : HALO - o + rows], axis=0, keepdims=True
        )
    dx = dx.astype(BF16)
    dx_ref[...] = dx
    all_ref[:, :wide] = dx
    all_ref[:, wide : wide + heads * val] = ggate_ref[...]
    all_ref[:, wide + heads * val :] = dsmall_ref[...]


def cost(micros):
    return pl.CostEstimate(flops=int(micros * 1.15e9), bytes_accessed=int(micros * 1e6), transcendentals=0)


def params():
    return pltpu.CompilerParams(dimension_semantics=("arbitrary",), vmem_limit_bytes=56 * 2**20)


def prepare(raw, small, taps, rates, lengths, heads, key, val, wait=()):
    length, width = raw.shape
    wide = heads * (2 * key + val)
    steps = length // ROWS
    ratio = ROWS // HALO
    row = lambda w: pl.BlockSpec((ROWS, w), lambda i: (i, 0))
    whole = lambda a: pl.BlockSpec(a.shape, lambda i: (0, 0))
    shape = lambda w, t: jax.ShapeDtypeStruct((length, w), t)
    kinds = [(wide, F32), (heads * key, BF16), (heads * key, BF16), (heads * key, BF16), (heads * val, F32),
             (heads * SPAN, F32), (heads * SPAN, BF16), (heads * SPAN, F32), (heads * SPAN, F32), (LANES, F32)]
    return pl.pallas_call(
        functools.partial(prepare_kernel, heads, key, val, len(wait)),
        grid=(steps,),
        in_specs=[
            pl.BlockSpec(memory_space=pltpu.SMEM),
            row(width),
            pl.BlockSpec((HALO, width), lambda i: (jnp.maximum(i * ratio - 1, 0), 0)),
            row(LANES),
            whole(taps),
            whole(rates),
        ] + [pl.BlockSpec(memory_space=pl.ANY)] * len(wait),
        out_specs=[row(w) for w, _ in kinds],
        out_shape=[shape(w, t) for w, t in kinds],
        compiler_params=params(),
        cost_estimate=cost(0.1),
        name="prepare",
    )(lengths, raw, raw, small, taps, rates, *wait)


def forward(qe, w, kd, fresh, p, cols, normed, gate_w, gain, heads, key, val, wait=()):
    length = qe.shape[0]
    steps = length // SPAN
    row = lambda a: pl.BlockSpec((SPAN, a.shape[1]), lambda i: (i, 0))
    given = [qe, w, kd, fresh, p, cols, normed]
    wide = heads * val
    kinds = [(wide, BF16), (wide, F32), (wide, BF16), (wide, BF16)]
    return pl.pallas_call(
        functools.partial(forward_kernel, heads, key, val, len(wait)),
        grid=(steps,),
        in_specs=[row(a) for a in given]
        + [pl.BlockSpec((gate_w.shape[0], wide), lambda i: (0, 0)), pl.BlockSpec(gain.shape, lambda i: (0, 0))]
        + [pl.BlockSpec(memory_space=pl.ANY)] * len(wait),
        out_specs=[pl.BlockSpec((SPAN, wd), lambda i: (i, 0)) for wd, _ in kinds]
        + [pl.BlockSpec((1, heads, key, val), lambda i: (i, 0, 0, 0))],
        out_shape=[jax.ShapeDtypeStruct((length, wd), t) for wd, t in kinds]
        + [jax.ShapeDtypeStruct((steps, heads, key, val), BF16)],
        scratch_shapes=[pltpu.VMEM((heads, key, val), F32)],
        compiler_params=params(),
        cost_estimate=cost(0.1),
        name="forward",
    )(*given, gate_w, gain, *wait)


def backward(grad, mixed, gate, gain, p, qe, w, kd, cols, heads, key, val, wait=()):
    length = qe.shape[0]
    steps = length // SPAN
    row = lambda a: pl.BlockSpec((SPAN, a.shape[1]), lambda i: (steps - 1 - i, 0))
    wide = heads * val
    kinds = [wide, wide, wide]
    back = pl.BlockSpec((SPAN, wide), lambda i: (steps - 1 - i, 0))
    full = jax.ShapeDtypeStruct((length, wide), BF16)
    return pl.pallas_call(
        functools.partial(backward_kernel, heads, key, val, len(wait)),
        grid=(steps,),
        in_specs=[row(grad), row(mixed), row(gate), pl.BlockSpec(gain.shape, lambda i: (0, 0)), row(p), row(qe), row(w),
                  row(kd), row(cols)] + [pl.BlockSpec(memory_space=pl.ANY)] * len(wait),
        out_specs=[back, pl.BlockSpec((1, val), lambda i: (0, 0)), back, back,
                   pl.BlockSpec((1, heads, key, val), lambda i: (steps - 1 - i, 0, 0, 0))],
        out_shape=[full, jax.ShapeDtypeStruct((1, val), F32), full, full,
                   jax.ShapeDtypeStruct((steps, heads, key, val), BF16)],
        scratch_shapes=[pltpu.VMEM((heads, key, val), F32)],
        compiler_params=params(),
        cost_estimate=cost(0.1),
        name="backward",
    )(grad, mixed, gate, gain, p, qe, w, kd, cols, *wait)


def finish(raw, taps, rates, lengths, u, p, t, decay, gram, cols, new, do, dn, ggate, enter, leave, heads, key, val, wait=()):
    length, width = raw.shape
    wide = heads * (2 * key + val)
    steps = length // ROWS
    ratio = ROWS // HALO
    per = ROWS // SPAN
    row = lambda a: pl.BlockSpec((ROWS, a.shape[1]), lambda i: (steps - 1 - i, 0))
    states = pl.BlockSpec((per, heads, key, val), lambda i: (steps - 1 - i, 0, 0, 0))
    whole = lambda a: pl.BlockSpec(a.shape, lambda i: (0, 0))
    fixed = lambda s: pl.BlockSpec(s, lambda i: (0, 0))
    given = [u, p, t, decay, gram, cols, new, do, dn, ggate]
    every = wide + heads * val + LANES
    out_row = lambda w: pl.BlockSpec((ROWS, w), lambda i: (steps - 1 - i, 0))
    return pl.pallas_call(
        functools.partial(finish_kernel, heads, key, val, len(wait)),
        grid=(steps,),
        in_specs=[
            pl.BlockSpec(memory_space=pltpu.SMEM),
            row(raw),
            pl.BlockSpec((HALO, width), lambda i: (jnp.maximum((steps - 1 - i) * ratio - 1, 0), 0)),
            whole(taps),
            whole(rates),
        ] + [row(a) for a in given] + [states, states] + [pl.BlockSpec(memory_space=pl.ANY)] * len(wait),
        out_specs=[out_row(wide), out_row(LANES), out_row(every), fixed((8, wide)), fixed((8, LANES))],
        out_shape=[*(jax.ShapeDtypeStruct((length, w), BF16) for w in (wide, LANES, every)), jax.ShapeDtypeStruct((8, wide), F32),
              jax.ShapeDtypeStruct((8, LANES), F32)],
        scratch_shapes=[pltpu.VMEM((ROWS + HALO, wide), F32)],
        compiler_params=params(),
        cost_estimate=cost(0.1),
        name="finish",
    )(lengths, raw, raw, taps, rates, *given, enter, leave, *wait)


def rows_kernel(order_ref, gain_ref, thin_ref, *refs):
    pieces, (normed_ref, logits_ref) = refs[:-2], refs[-2:]
    order, size = order_ref[...], pieces[0].shape[0]
    token = iota((order.shape[0], size), 1)
    rows = sum(
        jnp.dot((order == token + i * size).astype(BF16), piece[...], preferred_element_type=F32)
        for i, piece in enumerate(pieces)
    )
    scale = lax.rsqrt(lane_sum(rows * rows) * (1.0 / rows.shape[1]) + EPS)
    normed = (rows * scale * gain_ref[...]).astype(BF16)
    normed_ref[...] = normed
    logits_ref[...] = mm_bt(normed, thin_ref[...]).astype(BF16)


def packed_rows(order, gain, thin, pieces):
    length, size, wide = order.shape[0], 256, gain.shape[1]
    row = lambda w: pl.BlockSpec((size, w), lambda i: (i, 0))
    whole = lambda a: pl.BlockSpec(a.shape, lambda i: (0, 0))
    return pl.pallas_call(
        rows_kernel,
        grid=(length // size,),
        in_specs=[row(1), whole(gain), whole(thin)] + [whole(p) for p in pieces],
        out_specs=[row(wide), row(LANES)],
        out_shape=[jax.ShapeDtypeStruct((length, w), BF16) for w in (wide, LANES)],
        compiler_params=params(),
        cost_estimate=cost(26),
        name="packed_rows",
    )(order, gain, thin, *pieces)


def hidden_kernel(rows_ref, gate_ref, up_ref, grad_ref, act_ref, both_ref):
    rows = rows_ref[...]
    gating = jnp.dot(rows, gate_ref[...], preferred_element_type=F32)
    up = jnp.dot(rows, up_ref[...], preferred_element_type=F32)
    sig = 1.0 / (1.0 + jnp.exp(-gating))
    silu = gating * sig
    grad = grad_ref[...]
    act_ref[...] = (silu * up).astype(BF16)
    ggate = (grad * up * (sig + silu * (1.0 - sig))).astype(BF16)
    gup = (grad * silu).astype(BF16)
    both_ref[:, : ggate.shape[1]] = ggate
    both_ref[:, ggate.shape[1] :] = gup


def hidden_units(rows, gate, up, grad):
    (length, wide), units, size = rows.shape, gate.shape[1], 256
    row = lambda w: pl.BlockSpec((size, w), lambda i: (i, 0))
    weight = pl.BlockSpec(gate.shape, lambda i: (0, 0))
    return pl.pallas_call(
        hidden_kernel,
        grid=(length // size,),
        in_specs=[row(wide), weight, weight, row(units)],
        out_specs=[row(units), row(2 * units)],
        out_shape=[jax.ShapeDtypeStruct((length, w), BF16) for w in (units, 2 * units)],
        compiler_params=params(),
        cost_estimate=cost(0.1),
        name="hidden_units",
    )(rows, gate, up, grad)


def in_vmem(count):
    return [pl.BlockSpec(memory_space=pltpu.VMEM)] * count


def deal_kernel(n_parts, at, *refs):
    parts, outs = refs[:n_parts], refs[n_parts:]
    for d, out in enumerate(outs):
        for c in range(len(outs)):

            @pl.when((at[0] ^ d) == c)
            def _(out=out, c=c):
                begin = 0
                for part in parts:
                    width = part.shape[1] // len(outs)
                    out[:, begin : begin + width] = part[:, c * width : (c + 1) * width]
                    begin += width


def deal(at, parts, count):
    rows, width = parts[0].shape[0], sum(p.shape[1] for p in parts) // count
    return pl.pallas_call(
        functools.partial(deal_kernel, len(parts)),
        in_specs=[pl.BlockSpec(memory_space=pltpu.SMEM)] + in_vmem(len(parts)),
        out_specs=in_vmem(count),
        out_shape=[jax.ShapeDtypeStruct((rows, width), BF16)] * count,
        cost_estimate=cost(3),
        name="deal",
    )(at, *parts)


def stack_kernel(count, at, *refs):
    blocks, outs, rows = refs[:count], refs[count:], refs[0].shape[0]
    for d, block in enumerate(blocks):
        begin = 0
        for out in outs:
            width = out.shape[1]
            out[pl.ds(pl.multiple_of((at[0] ^ d) * rows, rows), rows), :] = block[:, begin : begin + width]
            begin += width


def stack(at, blocks, widths):
    rows = blocks[0].shape[0]
    return pl.pallas_call(
        functools.partial(stack_kernel, len(blocks)),
        in_specs=[pl.BlockSpec(memory_space=pltpu.SMEM)] + in_vmem(len(blocks)),
        out_specs=in_vmem(len(widths)),
        out_shape=[jax.ShapeDtypeStruct((len(blocks) * rows, w), BF16) for w in widths],
        cost_estimate=cost(2),
        name="stack",
    )(at, *blocks)


def collect_kernel(count, at, *refs):
    blocks, outs = refs[:count], refs[count:]
    for d, block in enumerate(blocks):
        for c in range(count):

            @pl.when((at[0] ^ d) == c)
            def _(block=block, c=c):
                begin = 0
                for out in outs:
                    width = out.shape[1] // count
                    out[:, c * width : (c + 1) * width] = block[:, begin : begin + width].astype(F32)
                    begin += width


def collect(at, blocks, widths):
    rows, count = blocks[0].shape[0], len(blocks)
    return pl.pallas_call(
        functools.partial(collect_kernel, count),
        in_specs=[pl.BlockSpec(memory_space=pltpu.SMEM)] + in_vmem(count),
        out_specs=in_vmem(len(widths)),
        out_shape=[jax.ShapeDtypeStruct((rows, w * count), F32) for w in widths],
        compiler_params=pltpu.CompilerParams(vmem_limit_bytes=32 * 2**20),
        cost_estimate=cost(2),
        name="collect",
    )(at, *blocks)


def tie_kernel(*refs):
    del refs


def tie(value, *earlier):
    anywhere = pl.BlockSpec(memory_space=pl.ANY)
    return pl.pallas_call(
        tie_kernel,
        in_specs=[anywhere] * (1 + len(earlier)),
        out_specs=anywhere,
        out_shape=jax.ShapeDtypeStruct(value.shape, value.dtype),
        input_output_aliases={0: 0},
        cost_estimate=cost(0.3),
        name="tie",
    )(value, *earlier)


def divide_kernel(count, at, *refs):
    parts, outs, rows = refs[:-count], refs[-count:], refs[-1].shape[0]
    for d, out in enumerate(outs):
        begin = 0
        for part in parts:
            width = part.shape[1]
            out[:, begin : begin + width] = part[pl.ds(pl.multiple_of((at[0] ^ d) * rows, rows), rows), :]
            begin += width


def divide(at, parts, count):
    rows, width = parts[0].shape[0] // count, sum(p.shape[1] for p in parts)
    return pl.pallas_call(
        functools.partial(divide_kernel, count),
        in_specs=[pl.BlockSpec(memory_space=pltpu.SMEM)] + in_vmem(len(parts)),
        out_specs=in_vmem(count),
        out_shape=[jax.ShapeDtypeStruct((rows, width), BF16)] * count,
        compiler_params=pltpu.CompilerParams(vmem_limit_bytes=32 * 2**20),
        cost_estimate=cost(3),
        name="divide",
    )(at, *parts)


def dense(a, b):
    return jnp.dot(a, b, preferred_element_type=F32)


def dense_t(a, b):
    return lax.dot_general(a, b, (((0,), (0,)), ((), ())), preferred_element_type=F32)


def dense_bt(a, b):
    return lax.dot_general(a, b, (((1,), (1,)), ((), ())), preferred_element_type=F32)


def flip(axis, distance, size):
    return lambda a: lax.ppermute(a, axis, [(i, i ^ distance) for i in range(size)])


def after(value, *earlier):
    return lax.optimization_barrier((value, *earlier))[0]


def local(
    residual, cotangent, lengths, token_order, norm_mixer, w_query, w_key, w_value, w_outgate, w_decay, w_beta,
    conv_query, conv_key, conv_value, decay_log, decay_bias, norm_head, w_output, norm_ffn, w_gate, w_up, w_down,
):
    n_ctx, n_tp = lax.axis_size("ctx"), lax.axis_size("tp")
    at_ctx, at_tp = lax.axis_index("ctx"), lax.axis_index("tp")
    rows_d = w_query.shape[0]
    heads = w_decay.shape[1] // n_ctx
    key = w_query.shape[1] // (n_ctx * heads)
    val = w_value.shape[1] // (n_ctx * heads)
    hk, hv = heads * key, heads * val
    wide = 2 * hk + hv
    units = w_gate.shape[1] // n_ctx
    group = token_order.shape[1]
    mine = group // (n_ctx * n_tp)

    across_core, across_x = flip("ctx", 1, n_ctx), flip("ctx", 2, n_ctx)
    across_both, across_y = flip("ctx", 3, n_ctx), flip("tp", 1, n_tp)
    half = mine // 2
    at_x, at_core = at_ctx // 2, at_ctx % 2

    def place_of(token):
        part, rest = token // half, token % half
        second, other_y = part % 2, (part // 2 % 2) ^ at_tp
        other_core, other_x = (part // 4 % 2) ^ at_core, (part // 8) ^ at_x
        pair = jnp.where(second == 1, other_y * 2 + other_x, other_x * 2 + other_y)
        return ((other_core * 2 + second) * 4 + pair) * half + rest

    def beside(*transfers):
        return lax.optimization_barrier(transfers)

    def place_given(token):
        part = (at_ctx ^ (token // (2 * mine)))
        return ((part % 2) * 2 + part // 2) * (2 * mine) + token % (2 * mine)

    def gather_tokens(block):
        first, second = block[:half], block[half:]
        first_y, second_x = beside(across_y(first), across_x(second))
        first = jnp.concatenate([first, first_y], axis=0)
        second = jnp.concatenate([second, second_x], axis=0)
        first_x, second_y = beside(across_x(first), across_y(second))
        chip = (first, first_x, second, second_y)
        return jnp.concatenate([*chip, *(across_core(piece) for piece in chip)], axis=0)

    def sort_given(near, far):
        def pick(block, second, other):
            return lax.dynamic_slice_in_dim(block, (at_tp ^ other) * mine + second * half, half, 0)

        def chip(near, far):
            return [
                *(pick(b, 0, other) for b in (near, far) for other in (0, 1)),
                *(pick(b, 1, other) for other in (0, 1) for b in (near, far)),
            ]

        return jnp.concatenate(chip(near, far) + chip(across_core(near), across_core(far)), axis=0)

    def product(*pairs):
        size = pairs[0][0].shape[0] // 4
        return [
            sum(dense_bt(rows[i * size : (i + 1) * size], matrix) for rows, matrix in pairs).astype(BF16)
            for i in (2, 3, 0, 1)
        ]

    def sum_cores(theirs_first, theirs_second, first, second):
        theirs_first, theirs_second = across_core(theirs_first), across_core(theirs_second)
        near, far = slice(0, 2 * half), slice(2 * half, 4 * half)
        return (
            both(first[near], theirs_first[near]), both(second[near], theirs_second[near]),
            both(first[far], theirs_first[far]).astype(BF16), both(second[far], theirs_second[far]).astype(BF16),
        )

    def sum_near(first, second, far_first, far_second):
        moved_first, moved_second = beside(across_x(far_first), across_y(far_second))
        first, second = both(first, moved_first), both(second, moved_second)
        return first[:half], second[:half], first[half:].astype(BF16), second[half:].astype(BF16)

    def sum_far(first, second, moved_first, moved_second):
        moved_first, moved_second = beside(across_y(moved_first), across_x(moved_second))
        return jnp.concatenate([both(first, moved_first), both(second, moved_second)], axis=0)

    def sum_tokens(*parts):
        return sum_far(*sum_near(*sum_cores(*parts)))

    def both(a, b):
        return a.astype(F32) + b.astype(F32)

    def pair_tokens(block):
        other = across_y(block)
        whole = jnp.concatenate([block, other], axis=0)
        swapped = jnp.concatenate([other, block], axis=0)
        return jnp.where(at_tp == 0, whole, swapped)

    at_here = jnp.reshape(at_ctx, (1,)).astype(jnp.int32)

    def exchange(blocks):
        return [blocks[0], across_core(blocks[1]), across_x(blocks[2]), across_both(blocks[3])]

    def spread(place, *parts):
        blocks = exchange(deal(place, parts, n_ctx))
        return stack(at_here, blocks, (blocks[0].shape[1],))[0]

    def every(block):
        return lax.all_gather(block, "fsdp", axis=0, tiled=True)

    def reduce(partial):
        return lax.psum_scatter(partial, "fsdp", scatter_dimension=0, tiled=True)

    def own(place, blocks, *widths):
        return collect(at_here, exchange(divide(place, blocks, n_ctx)), widths)

    def vectors(block):
        n_groups, count, distance = lax.axis_size("fsdp"), block.shape[0], 1
        places = []
        for move, place in ((across_core, at_core), (across_x, at_x)):
            block, places = jnp.stack([block, move(block)]), [place, *places]
        while distance < n_groups:
            block = jnp.stack([block, flip("fsdp", distance, n_groups)(block)])
            places = [lax.axis_index("fsdp") // distance % 2, *places]
            distance *= 2
        moved = block
        for axis, place in enumerate(places):
            block = jnp.where(place == 0, block, jnp.flip(block, axis))
        return jnp.moveaxis(block.reshape(-1, count, block.shape[-1]), 1, 0).reshape(count, -1), moved

    first_in = spread(at_here, w_query, w_key, w_value)
    w_first = every(first_in)
    thin, thin_moved = vectors(jnp.concatenate([norm_mixer[None], norm_ffn[None], w_decay.T, w_beta.T], axis=0))
    n_mix, n_ffn = thin[0].astype(F32), thin[1].astype(F32)
    w_thin = jnp.concatenate([
        lax.dynamic_slice_in_dim(thin, 2 + at_ctx * heads, heads, 0),
        lax.dynamic_slice_in_dim(thin, 2 + (n_ctx + at_ctx) * heads, heads, 0),
    ])
    w_thin = jnp.pad(w_thin, ((0, LANES - 2 * heads), (0, 0)))
    source_in = lax.dynamic_slice_in_dim(residual, at_tp * mine, mine, 0)
    near = tie(residual, first_in, thin_moved)
    far = across_x(near)
    tokens = (near, far, across_core(near), across_core(far))
    order = place_of(token_order[0])
    inverse = jnp.zeros_like(order).at[order].set(lax.iota(jnp.int32, group))
    second_in = spread(tie(at_here, far, thin, inverse), w_outgate, w_output.T)
    w_second = every(second_in)
    w_gates, w_out = w_second[:, :hv], w_second[:, hv:]
    normed1, raw_thin = packed_rows(place_given(token_order[0])[:, None], n_mix[None], w_thin, tokens)
    cot_in = lax.dynamic_slice_in_dim(cotangent, at_tp * mine, mine, 0)
    raw = dense(normed1, w_first).astype(BF16)
    cot_far = across_x(tie(cotangent, raw))
    cot = sort_given(cotangent, cot_far)
    later = tie(at_here, raw)
    last_in, gate_in, up_in = spread(later, w_down.T), spread(later, w_gate), spread(later, w_up)
    w_last, w_gating, w_uppart = every(last_in), every(gate_in), every(up_in)

    first_head = (at_tp * n_ctx + at_ctx) * heads

    def share(conv, width):
        return lax.dynamic_slice_in_dim(conv.astype(F32), first_head * width, heads * width, 1)

    taps = jnp.concatenate([share(conv_query, key), share(conv_key, key), share(conv_value, val)], axis=1)
    taps = jnp.concatenate([taps, jnp.zeros_like(taps)], axis=0)
    rates = jnp.stack([
        lax.dynamic_slice_in_dim(decay_log, first_head, heads, 0),
        lax.dynamic_slice_in_dim(decay_bias, first_head, heads, 0),
    ])
    rates = jnp.pad(rates, ((0, 6), (0, LANES - heads)))
    gain = norm_head.astype(F32)[None, :]
    sizes = (heads, key, val)
    u, qe, wm, kd, fresh, p, solve, decay, gram, cols = prepare(
        raw, raw_thin, taps, rates, lengths, *sizes, wait=(second_in,)
    )
    headout, mixed, new, gate, enter = forward(
        qe, wm, kd, fresh, p, cols, normed1, w_second, gain, *sizes, wait=(last_in, gate_in)
    )

    given = headout[tie(inverse, cot_far, up_in)]
    attention = sum_tokens(*product((given, w_out)))
    source = source_in.astype(F32)
    middle = source + attention
    scale2 = lax.rsqrt(jnp.mean(middle * middle, axis=-1, keepdims=True) + EPS)
    grad_act = dense(cot, w_last)
    normed2 = (middle * scale2 * n_ffn).astype(BF16)
    normed2 = gather_tokens(tie(normed2, grad_act, w_gating))
    w_hidden = jnp.concatenate([w_gating, w_uppart], axis=1)
    activation, grad_hidden = hidden_units(normed2, w_gating, w_uppart, grad_act)
    g_last = dense_t(cot, activation).astype(BF16)
    grad_hidden = tie(grad_hidden, g_last)
    g_last = reduce(g_last)
    grad_parts = product((grad_hidden, w_hidden))
    grad_normed2 = sum_tokens(*grad_parts)
    g_hidden = dense_t(tie(normed2, *grad_parts), grad_hidden).astype(BF16)

    def norm_back(u_in, s, n, g):
        weighted = n * g
        return s * weighted - u_in * (s * s * s) * jnp.mean(u_in * weighted, axis=-1, keepdims=True)

    grad_mid = cot_in.astype(F32) + norm_back(middle, scale2, n_ffn, grad_normed2)
    ffn_parts = product((activation, w_last))
    w_all = jnp.concatenate([w_first, w_gates, w_thin.T], axis=1)
    grad_attn = gather_tokens(tie(grad_mid.astype(BF16), *ffn_parts, g_hidden, g_last, w_all))
    g_hidden = reduce(g_hidden)
    grad_given = dense(grad_attn, w_out).astype(BF16)

    ffn_send = sum_cores(tie(ffn_parts[0], grad_attn), tie(ffn_parts[1], grad_attn), *ffn_parts[2:])
    ffn_near = sum_near(*ffn_send)
    grad_gate, g_gain, do, dn, leave = backward(
        grad_given[tie(order, ffn_send[2], ffn_send[3])], mixed, gate, gain, p, qe, wm, kd, cols, *sizes
    )
    g_out = reduce(dense_t(grad_attn, tie(given, grad_gate)).astype(BF16))
    g_gates = dense_t(normed1, grad_gate).astype(BF16)
    ffn_out = sum_far(*ffn_near)
    dx, dx_thin, dx_all, g_taps, g_small = finish(
        raw, taps, rates, lengths, u, p, solve, decay, gram, cols, new, do, dn, grad_gate, enter, leave, *sizes,
        wait=(g_gates, *ffn_near[2:], g_hidden),
    )
    g_gates = reduce(g_gates)
    output = pair_tokens((middle + ffn_out).astype(BF16))
    g_first = dense_t(normed1, tie(dx, ffn_out)).astype(BF16)
    inverse = tie(inverse, g_first, g_out)
    g_first = reduce(g_first)
    grad_parts = product((tie(dx_all[inverse], output), w_all))
    later = tie(at_here, grad_parts[3])
    g_taps = tie(g_taps, grad_parts[3])
    grad_normed1 = sum_tokens(*grad_parts)
    scale1 = lax.rsqrt(jnp.mean(source * source, axis=-1, keepdims=True) + EPS)
    grad_input = (grad_mid + norm_back(source, scale1, n_mix, grad_normed1)).astype(BF16)
    grad_input = pair_tokens(grad_input)

    gw_gate, gw_up, gw_down = own(later, (g_hidden, g_last), units, units, units)
    gw_query, gw_key, gw_value, gw_output, gw_outgate = own(
        tie(at_here, grad_normed1), (g_first, g_out, g_gates), hk, hk, hv, hv, hv
    )
    gw_output, gw_down = gw_output.T, gw_down.T

    def pad(vector):
        return jnp.pad(vector, (0, -vector.size % LANES)).reshape(-1, LANES)

    g_thin = dense_t(dx_thin, normed1)[: 2 * heads].reshape(-1, LANES)
    sums = jnp.concatenate([g_taps[:TAPS].reshape(-1, LANES), pad(g_gain[0]), g_small[:2], g_thin], axis=0)
    n_groups, distance = lax.axis_size("fsdp"), 1
    while distance < n_groups:
        sums = sums + flip("fsdp", distance, n_groups)(sums)
        distance *= 2
    for move in (across_y, across_x, across_core):
        sums = jnp.stack([sums, move(sums)])
    sums = sums.reshape(2, 2, 2, *sums.shape[3:])
    sums = jnp.where(at_core == 0, sums, sums[::-1])
    sums = jnp.where(at_x == 0, sums, sums[:, ::-1])
    sums = jnp.where(at_tp == 0, sums, sums[:, :, ::-1])
    sums = sums.transpose(2, 1, 0, 3, 4).reshape(n_tp * n_ctx, *sums.shape[3:])
    of_taps = TAPS * wide // LANES
    of_thin = g_thin.shape[0]
    tap_sums = sums[:, :of_taps].reshape(-1, TAPS, wide).swapaxes(0, 1)

    def heads_of(begin, end):
        return tap_sums[:, :, begin:end].reshape(TAPS, -1)

    pieces = (
        heads_of(0, hk), heads_of(hk, 2 * hk), heads_of(2 * hk, wide),
        sums[:, -2 - of_thin, :heads].reshape(-1), sums[:, -1 - of_thin, :heads].reshape(-1),
        jnp.sum(sums[:, of_taps : -2 - of_thin], axis=0).reshape(-1)[:val],
    )
    thin_sums = sums[:, -of_thin:].reshape(n_tp, n_ctx, 2, heads, n_ctx * lax.axis_size("fsdp"), rows_d)
    thin_sums = lax.dynamic_index_in_dim(thin_sums, at_tp, 0, keepdims=False)
    thin_sums = lax.dynamic_index_in_dim(thin_sums, lax.axis_index("fsdp") * n_ctx + at_ctx, 3, keepdims=False)
    gw_decay = thin_sums[:, 0].reshape(-1, rows_d).T
    gw_beta = thin_sums[:, 1].reshape(-1, rows_d).T

    def overlap(*pairs):
        return sum(jnp.sum(w.astype(F32) * g, axis=1) for w, g in pairs)

    g_norms = jnp.stack([
        overlap((w_query, gw_query), (w_key, gw_key), (w_value, gw_value), (w_outgate, gw_outgate),
                (w_decay, gw_decay), (w_beta, gw_beta)) / norm_mixer.astype(F32),
        overlap((w_gate, gw_gate), (w_up, gw_up)) / norm_ffn.astype(F32),
    ])
    g_norms = g_norms + across_y(g_norms)

    return (
        output, grad_input, g_norms[0], gw_query, gw_key, gw_value, gw_outgate, gw_decay, gw_beta,
        *pieces, gw_output, g_norms[1], gw_gate, gw_up, gw_down,
    )


def solution(mesh):
    rows = ("fsdp", "ctx")
    up, down, vector, copied = P(rows, "tp"), P("tp", rows), P(rows), P()
    in_specs = (
        P(rows, None), P(rows, None), P("fsdp", None), P("fsdp", None), vector, up, up, up, up, up, up,
        copied, copied, copied, copied, copied, copied, down, vector, up, up, down,
    )
    out_specs = (
        P(rows, None), P(rows, None), vector, up, up, up, up, up, up,
        copied, copied, copied, copied, copied, copied, down, vector, up, up, down,
    )
    return jax.shard_map(local, mesh=mesh, in_specs=in_specs, out_specs=out_specs, check_vma=False)
```

```python
import functools
import jax
import jax.numpy as jnp
from jax import lax
from jax.experimental import pallas as pl
from jax.experimental.pallas import tpu as pltpu
from jax.sharding import PartitionSpec as P

EPS = 1e-06
HEAD_FLOOR = 0.01
SPAN = 128
ROWS = 256
HALO = 16
TAPS = 4
LANES = 128
F32 = jnp.float32
BF16 = jnp.bfloat16
HIGHEST = lax.Precision.HIGHEST


def mm(a, b):
    return lax.dot_general(a.astype(BF16), b.astype(BF16), (((1,), (0,)), ((), ())), preferred_element_type=F32)


def mm_bt(a, b):
    return lax.dot_general(a.astype(BF16), b.astype(BF16), (((1,), (1,)), ((), ())), preferred_element_type=F32)


def mm_at(a, b):
    return lax.dot_general(a.astype(BF16), b.astype(BF16), (((0,), (0,)), ((), ())), preferred_element_type=F32)


def exact(a, b):
    return jnp.dot(a, b, precision=HIGHEST, preferred_element_type=F32)


def iota(shape, axis):
    return lax.broadcasted_iota(jnp.int32, shape, axis)


def bounds_of(lengths):
    found, total = [], 0
    for s in range(lengths.shape[1] - 1):
        total = total + lengths[0, s]
        found.append(total)
    return found


def begin_of(rows, bounds):
    begin = jnp.zeros_like(rows)
    for edge in bounds:
        begin = jnp.where(rows >= edge, edge, begin)
    return begin


def lane_sum(value):
    return jnp.sum(value, axis=1, keepdims=True)


def at_lane(lane, place, column):
    return jnp.where(lane == place, column, 0.0)


def invert(lower):
    size = lower.shape[0]
    row, col = iota((size, size), 0), iota((size, size), 1)
    inverse = jnp.where(row == col, 1.0, jnp.where(row // 2 == col // 2, -lower, 0.0))
    width = 2
    while width < size:
        joint = (row // (2 * width) == col // (2 * width)) & (row // width != col // width)
        between = jnp.where(joint, lower, 0.0)
        held = inverse.astype(BF16)
        inverse = inverse - mm(mm(held, between), held)
        width *= 2
    return inverse


def conv_rows(before, block, taps, pos):
    ext = jnp.concatenate([before, block], axis=0)
    size = block.shape[0]
    total = taps[0:1] * block
    for o in range(1, TAPS):
        total = total + jnp.where(pos >= o, taps[o : o + 1], 0.0) * ext[HALO - o : HALO - o + size]
    return total


def prepare_kernel(heads, key, val, n_wait, lengths, raw_ref, before_ref, small_ref, taps_ref, rate_ref, *refs):
    prepare_block(heads, key, val, lengths, raw_ref, before_ref, small_ref, taps_ref, rate_ref, *refs[n_wait:])


def prepare_block(heads, key, val, lengths, raw_ref, before_ref, small_ref, taps_ref, rate_ref,
                   u_ref, qe_ref, w_ref, kd_ref, fresh_ref, p_ref, t_ref, decay_ref, gram_ref, cols_ref):
    rows = raw_ref.shape[0]
    first = pl.program_id(0) * rows
    bounds = bounds_of(lengths)
    where_row = first + iota((rows, 1), 0)
    begin = begin_of(where_row, bounds)
    pos = where_row - begin
    u = conv_rows(before_ref[...].astype(F32), raw_ref[...].astype(F32), taps_ref[...], pos)
    u_ref[...] = u
    act = u / (1.0 + jnp.exp(-u))
    small = small_ref[...].astype(F32)
    lane = iota((SPAN, LANES), 1)
    row_i, col_i = iota((SPAN, SPAN), 0), iota((SPAN, SPAN), 1)
    tri = (row_i >= col_i).astype(F32)
    for c in range(rows // SPAN):
        at = slice(c * SPAN, (c + 1) * SPAN)
        base = first + c * SPAN
        begin_c = begin[at]
        begin_r = begin_of(base + iota((1, SPAN), 1), bounds)
        last_begin = begin_of(base + SPAN - 1 + iota((1, 1), 0), bounds)
        shifted = small[at] + rate_ref[1:2]
        soft = jnp.maximum(shifted, 0.0) + jnp.log(1.0 + jnp.exp(-jnp.abs(shifted)))
        slope = 1.0 / (1.0 + jnp.exp(-shifted))
        logd = jnp.where(lane < heads, -jnp.exp(rate_ref[0:1]) * soft, 0.0)
        beta = 1.0 / (1.0 + jnp.exp(-small[at]))
        total = exact(tri, logd)
        total_t = jnp.transpose(total)
        last = total[SPAN - 1 : SPAN]
        reach = jnp.where(begin_c < base, jnp.exp(total), 0.0)
        tail = jnp.where(begin_c == last_begin, jnp.exp(jnp.where(begin_c == last_begin, last - total, 0.0)), 0.0)
        keep = jnp.where(last_begin < base, jnp.exp(last), 0.0)
        two = heads
        cols_ref[at] = (
            jnp.where(lane < two, reach, 0.0)
            + jnp.where((lane >= two) & (lane < 2 * two), beta, 0.0)
            + pltpu.roll(jnp.where(lane < two, tail, 0.0), 2 * two, 1)
            + pltpu.roll(logd, 3 * two, 1)
            + pltpu.roll(jnp.where(lane < two, keep, 0.0), 4 * two, 1)
            + pltpu.roll(jnp.where(lane < two, slope, 0.0), 5 * two, 1)
        )
        same = begin_c == begin_r
        upto = same & (row_i >= col_i)
        for h in range(heads):
            q = act[at, h * key : (h + 1) * key]
            k = act[at, (heads + h) * key : (heads + h + 1) * key]
            v = act[at, 2 * heads * key + h * val : 2 * heads * key + (h + 1) * val]
            q = q * lax.rsqrt(lane_sum(q * q) + EPS)
            k = k * lax.rsqrt(lane_sum(k * k) + EPS)
            b = beta[:, heads + h : heads + h + 1]
            r = reach[:, h : h + 1]
            spread = total[:, h : h + 1] - total_t[h : h + 1]
            decay = jnp.where(upto, jnp.exp(jnp.where(upto, spread, 0.0)), 0.0)
            both = mm_bt(jnp.concatenate([q, k], axis=0), k)
            gram = jnp.where(row_i > col_i, both[SPAN:] * decay, 0.0)
            inverse = invert(b * gram).astype(BF16)
            kat = slice(h * key, (h + 1) * key)
            cat = slice(h * SPAN, (h + 1) * SPAN)
            vat = slice(h * val, (h + 1) * val)
            solved = mm(inverse, jnp.concatenate([b * v, (b * r) * k], axis=1))
            fresh_ref[at, vat] = solved[:, :val]
            w_ref[at, kat] = solved[:, val:].astype(BF16)
            qe_ref[at, kat] = (r * q).astype(BF16)
            kd_ref[at, kat] = (tail[:, h : h + 1] * k).astype(BF16)
            p_ref[at, cat] = both[:SPAN] * decay
            t_ref[at, cat] = inverse
            decay_ref[at, cat] = decay
            gram_ref[at, cat] = gram


def forward_kernel(heads, key, val, n_wait, qe_ref, w_ref, kd_ref, fresh_ref, p_ref, cols_ref, normed_ref, gate_w_ref,
                   gain_ref, *refs):
    out_ref, mixed_ref, new_ref, gate_ref, enter_ref, state = refs[n_wait:]

    @pl.when(pl.program_id(0) == 0)
    def _():
        state[...] = jnp.zeros_like(state)

    gates = mm(normed_ref[...], gate_w_ref[...]).astype(BF16)
    gate_ref[...] = gates
    for h in range(heads):
        kat = slice(h * key, (h + 1) * key)
        cat = slice(h * SPAN, (h + 1) * SPAN)
        vat = slice(h * val, (h + 1) * val)
        carried = state[h]
        low = carried.astype(BF16)
        enter_ref[0, h] = low
        through = mm(jnp.concatenate([w_ref[:, kat], qe_ref[:, kat]], axis=0), low)
        new = (fresh_ref[:, vat] - through[:SPAN]).astype(BF16)
        new_ref[:, vat] = new
        keep = cols_ref[0:1, 4 * heads + h : 4 * heads + h + 1]
        state[h] = keep * carried + mm_at(kd_ref[:, kat], new)
        mixed = through[SPAN:] + mm(p_ref[:, cat], new)
        mixed_ref[:, vat] = mixed
        gate = gates[:, vat].astype(F32)
        scale = lax.rsqrt(lane_sum(mixed * mixed) * (1.0 / val) + HEAD_FLOOR)
        out_ref[:, vat] = (mixed * scale * gain_ref[...] * (gate / (1.0 + jnp.exp(-gate)))).astype(BF16)


def backward_kernel(heads, key, val, n_wait, grad_ref, mixed_ref, gate_ref, gain_ref, p_ref, qe_ref, w_ref, kd_ref,
                    cols_ref, *refs):
    ggate_ref, gain_out_ref, do_ref, dn_ref, leave_ref, state = refs[n_wait:]

    @pl.when(pl.program_id(0) == 0)
    def _():
        state[...] = jnp.zeros_like(state)
        gain_out_ref[...] = jnp.zeros_like(gain_out_ref)

    for h in range(heads):
        kat = slice(h * key, (h + 1) * key)
        cat = slice(h * SPAN, (h + 1) * SPAN)
        vat = slice(h * val, (h + 1) * val)
        grad = grad_ref[:, vat].astype(F32)
        mixed = mixed_ref[:, vat]
        gate = gate_ref[:, vat].astype(F32)
        gain = gain_ref[...]
        scale = lax.rsqrt(lane_sum(mixed * mixed) * (1.0 / val) + HEAD_FLOOR)
        sig = 1.0 / (1.0 + jnp.exp(-gate))
        silu = gate * sig
        normed = mixed * scale
        ggate_ref[:, vat] = (grad * normed * gain * (sig + silu * (1.0 - sig))).astype(BF16)
        gs = grad * silu
        gain_out_ref[...] += jnp.sum(gs * normed, axis=0, keepdims=True)
        weighted = gs * gain
        do = scale * (weighted - normed * (lane_sum(weighted * normed) * (1.0 / val)))
        do = do.astype(BF16)
        do_ref[:, vat] = do
        carried = state[h]
        low = carried.astype(BF16)
        leave_ref[0, h] = low
        dn = (mm_at(p_ref[:, cat], do) + mm(kd_ref[:, kat], low)).astype(BF16)
        dn_ref[:, vat] = dn
        keep = cols_ref[0:1, 4 * heads + h : 4 * heads + h + 1]
        state[h] = keep * carried + mm_at(
            jnp.concatenate([qe_ref[:, kat], -w_ref[:, kat]], axis=0), jnp.concatenate([do, dn], axis=0)
        )


def finish_kernel(heads, key, val, n_wait, lengths, raw_ref, before_ref, taps_ref, rate_ref, u_ref, p_ref, t_ref, decay_ref,
                  gram_ref, cols_ref, new_ref, do_ref, dn_ref, ggate_ref, enter_ref, leave_ref, *refs):
    dx_ref, dsmall_ref, all_ref, gtaps_ref, gsmall_ref, du_ref = refs[n_wait:]
    wide = heads * (2 * key + val)
    rows = raw_ref.shape[0]
    block = pl.num_programs(0) - 1 - pl.program_id(0)
    first = block * rows
    bounds = bounds_of(lengths)

    @pl.when(pl.program_id(0) == 0)
    def _():
        du_ref[rows:] = jnp.zeros((HALO, wide), F32)
        gtaps_ref[...] = jnp.zeros_like(gtaps_ref)
        gsmall_ref[...] = jnp.zeros_like(gsmall_ref)

    @pl.when(pl.program_id(0) > 0)
    def _():
        du_ref[rows:] = du_ref[:HALO]

    lane = iota((SPAN, LANES), 1)
    row_i, col_i = iota((SPAN, SPAN), 0), iota((SPAN, SPAN), 1)
    tri_up = (row_i <= col_i).astype(F32)
    row_c = iota((SPAN, 1), 0)

    def unit(u):
        sig = 1.0 / (1.0 + jnp.exp(-u))
        act = u * sig
        inv = lax.rsqrt(lane_sum(act * act) + EPS)
        return act * inv, inv, sig * (1.0 + u * (1.0 - sig))

    for c in range(rows // SPAN):
        at = slice(c * SPAN, (c + 1) * SPAN)
        cols = cols_ref[at]
        gtotal = jnp.zeros((SPAN, LANES), F32)
        gcross = jnp.zeros((SPAN, SPAN), F32)
        gbeta = jnp.zeros((SPAN, LANES), F32)
        for h in range(heads):
            qat = slice(h * key, (h + 1) * key)
            kat = slice((heads + h) * key, (heads + h + 1) * key)
            xat = slice(2 * heads * key + h * val, 2 * heads * key + (h + 1) * val)
            cat = slice(h * SPAN, (h + 1) * SPAN)
            vat = slice(h * val, (h + 1) * val)
            reach = cols[:, h : h + 1]
            beta = cols[:, heads + h : heads + h + 1]
            tail = cols[:, 2 * heads + h : 2 * heads + h + 1]
            keep = cols[0:1, 4 * heads + h : 4 * heads + h + 1]
            q, q_inv, q_slope = unit(u_ref[at, qat])
            k, k_inv, k_slope = unit(u_ref[at, kat])
            qb, kb = q.astype(BF16), k.astype(BF16)
            new, do = new_ref[at, vat], do_ref[at, vat]
            enter, leave = enter_ref[c, h], leave_ref[c, h]
            decay, gram = decay_ref[at, cat], gram_ref[at, cat]
            dr = mm_at(t_ref[at, cat], dn_ref[at, vat])
            stacked = jnp.concatenate([do, dr.astype(BF16)], axis=0)
            on_new = mm_bt(stacked, new)
            on_state = mm_bt(stacked, enter)
            dp, dl = on_new[:SPAN], -on_new[SPAN:]
            dqe, drs = on_state[:SPAN], on_state[SPAN:]
            dkd = mm_bt(new, leave)
            dpd = (dp * decay).astype(BF16)
            dkk = jnp.where(row_i > col_i, dl * (beta * decay), 0.0)
            dlg = dl * gram
            change = dp * p_ref[at, cat] + beta * dlg
            dq = reach * dqe + mm(dpd, kb)
            dk = (
                tail * dkd
                - (beta * reach) * drs
                + mm(dkk + jnp.transpose(dkk), kb)
                + mm_at(dpd, qb)
            )
            u_v = u_ref[at, xat]
            v_sig = 1.0 / (1.0 + jnp.exp(-u_v))
            v = u_v * v_sig
            drs_k = lane_sum(drs * k)
            dtail = lane_sum(dkd * k) * tail
            gb = lane_sum(dr * v) - reach * drs_k + lane_sum(dlg)
            dlast = jnp.sum(dtail, axis=0, keepdims=True) + keep * jnp.sum(
                lane_sum(enter.astype(F32) * leave.astype(F32)), axis=0, keepdims=True
            )
            gt = lane_sum(change) + reach * (lane_sum(dqe * q) - beta * drs_k) - dtail
            gt = gt + jnp.where(row_c == SPAN - 1, dlast, 0.0)
            gtotal = gtotal + at_lane(lane, h, gt)
            gcross = gcross + jnp.where(row_i == h, jnp.sum(change, axis=0, keepdims=True), 0.0)
            gbeta = gbeta + at_lane(lane, heads + h, gb * beta * (1.0 - beta))
            du_ref[at, qat] = q_inv * (dq - q * lane_sum(dq * q)) * q_slope
            du_ref[at, kat] = k_inv * (dk - k * lane_sum(dk * k)) * k_slope
            du_ref[at, xat] = (beta * dr) * (v_sig * (1.0 + u_v * (1.0 - v_sig)))
        glog = exact(tri_up, gtotal - jnp.transpose(gcross))
        logd = jnp.where(lane < heads, pltpu.roll(cols, LANES - 3 * heads, 1), 0.0)
        slope = jnp.where(lane < heads, pltpu.roll(cols, LANES - 5 * heads, 1), 0.0)
        gdecay = -glog * jnp.exp(rate_ref[0:1]) * slope
        gsmall_ref[0:1] += jnp.sum(glog * logd, axis=0, keepdims=True)
        gsmall_ref[1:2] += jnp.sum(gdecay, axis=0, keepdims=True)
        dsmall_ref[at] = (gdecay + gbeta).astype(BF16)
    where_row = first + iota((rows, 1), 0)
    pos = where_row - begin_of(where_row, bounds)
    ext = jnp.concatenate([before_ref[...].astype(F32), raw_ref[...].astype(F32)], axis=0)
    du = du_ref[:rows]
    dx = taps_ref[0:1] * du
    gtaps_ref[0:1] += jnp.sum(du * ext[HALO:], axis=0, keepdims=True)
    for o in range(1, TAPS):
        ahead = where_row + o
        pos_ahead = ahead - begin_of(ahead, bounds)
        dx = dx + jnp.where(pos_ahead >= o, taps_ref[o : o + 1], 0.0) * du_ref[o : o + rows]
        gtaps_ref[o : o + 1] += jnp.sum(
            jnp.where(pos >= o, du, 0.0) * ext[HALO - o : HALO - o + rows], axis=0, keepdims=True
        )
    dx = dx.astype(BF16)
    dx_ref[...] = dx
    all_ref[:, :wide] = dx
    all_ref[:, wide : wide + heads * val] = ggate_ref[...]
    all_ref[:, wide + heads * val :] = dsmall_ref[...]


def cost(micros):
    return pl.CostEstimate(flops=int(micros * 1.15e9), bytes_accessed=int(micros * 1e6), transcendentals=0)


def params():
    return pltpu.CompilerParams(dimension_semantics=("arbitrary",), vmem_limit_bytes=56 * 2**20)


def prepare(raw, small, taps, rates, lengths, heads, key, val, wait=()):
    length, width = raw.shape
    wide = heads * (2 * key + val)
    steps = length // ROWS
    ratio = ROWS // HALO
    row = lambda w: pl.BlockSpec((ROWS, w), lambda i: (i, 0))
    whole = lambda a: pl.BlockSpec(a.shape, lambda i: (0, 0))
    shape = lambda w, t: jax.ShapeDtypeStruct((length, w), t)
    kinds = [(wide, F32), (heads * key, BF16), (heads * key, BF16), (heads * key, BF16), (heads * val, F32),
             (heads * SPAN, F32), (heads * SPAN, BF16), (heads * SPAN, F32), (heads * SPAN, F32), (LANES, F32)]
    return pl.pallas_call(
        functools.partial(prepare_kernel, heads, key, val, len(wait)),
        grid=(steps,),
        in_specs=[
            pl.BlockSpec(memory_space=pltpu.SMEM),
            row(width),
            pl.BlockSpec((HALO, width), lambda i: (jnp.maximum(i * ratio - 1, 0), 0)),
            row(LANES),
            whole(taps),
            whole(rates),
        ] + [pl.BlockSpec(memory_space=pl.ANY)] * len(wait),
        out_specs=[row(w) for w, _ in kinds],
        out_shape=[shape(w, t) for w, t in kinds],
        compiler_params=params(),
        cost_estimate=cost(0.1),
        name="prepare",
    )(lengths, raw, raw, small, taps, rates, *wait)


def forward(qe, w, kd, fresh, p, cols, normed, gate_w, gain, heads, key, val, wait=()):
    length = qe.shape[0]
    steps = length // SPAN
    row = lambda a: pl.BlockSpec((SPAN, a.shape[1]), lambda i: (i, 0))
    given = [qe, w, kd, fresh, p, cols, normed]
    wide = heads * val
    kinds = [(wide, BF16), (wide, F32), (wide, BF16), (wide, BF16)]
    return pl.pallas_call(
        functools.partial(forward_kernel, heads, key, val, len(wait)),
        grid=(steps,),
        in_specs=[row(a) for a in given]
        + [pl.BlockSpec((gate_w.shape[0], wide), lambda i: (0, 0)), pl.BlockSpec(gain.shape, lambda i: (0, 0))]
        + [pl.BlockSpec(memory_space=pl.ANY)] * len(wait),
        out_specs=[pl.BlockSpec((SPAN, wd), lambda i: (i, 0)) for wd, _ in kinds]
        + [pl.BlockSpec((1, heads, key, val), lambda i: (i, 0, 0, 0))],
        out_shape=[jax.ShapeDtypeStruct((length, wd), t) for wd, t in kinds]
        + [jax.ShapeDtypeStruct((steps, heads, key, val), BF16)],
        scratch_shapes=[pltpu.VMEM((heads, key, val), F32)],
        compiler_params=params(),
        cost_estimate=cost(0.1),
        name="forward",
    )(*given, gate_w, gain, *wait)


def backward(grad, mixed, gate, gain, p, qe, w, kd, cols, heads, key, val, wait=()):
    length = qe.shape[0]
    steps = length // SPAN
    row = lambda a: pl.BlockSpec((SPAN, a.shape[1]), lambda i: (steps - 1 - i, 0))
    wide = heads * val
    kinds = [wide, wide, wide]
    back = pl.BlockSpec((SPAN, wide), lambda i: (steps - 1 - i, 0))
    full = jax.ShapeDtypeStruct((length, wide), BF16)
    return pl.pallas_call(
        functools.partial(backward_kernel, heads, key, val, len(wait)),
        grid=(steps,),
        in_specs=[row(grad), row(mixed), row(gate), pl.BlockSpec(gain.shape, lambda i: (0, 0)), row(p), row(qe), row(w),
                  row(kd), row(cols)] + [pl.BlockSpec(memory_space=pl.ANY)] * len(wait),
        out_specs=[back, pl.BlockSpec((1, val), lambda i: (0, 0)), back, back,
                   pl.BlockSpec((1, heads, key, val), lambda i: (steps - 1 - i, 0, 0, 0))],
        out_shape=[full, jax.ShapeDtypeStruct((1, val), F32), full, full,
                   jax.ShapeDtypeStruct((steps, heads, key, val), BF16)],
        scratch_shapes=[pltpu.VMEM((heads, key, val), F32)],
        compiler_params=params(),
        cost_estimate=cost(0.1),
        name="backward",
    )(grad, mixed, gate, gain, p, qe, w, kd, cols, *wait)


def finish(raw, taps, rates, lengths, u, p, t, decay, gram, cols, new, do, dn, ggate, enter, leave, heads, key, val, wait=()):
    length, width = raw.shape
    wide = heads * (2 * key + val)
    steps = length // ROWS
    ratio = ROWS // HALO
    per = ROWS // SPAN
    row = lambda a: pl.BlockSpec((ROWS, a.shape[1]), lambda i: (steps - 1 - i, 0))
    states = pl.BlockSpec((per, heads, key, val), lambda i: (steps - 1 - i, 0, 0, 0))
    whole = lambda a: pl.BlockSpec(a.shape, lambda i: (0, 0))
    fixed = lambda s: pl.BlockSpec(s, lambda i: (0, 0))
    given = [u, p, t, decay, gram, cols, new, do, dn, ggate]
    every = wide + heads * val + LANES
    out_row = lambda w: pl.BlockSpec((ROWS, w), lambda i: (steps - 1 - i, 0))
    return pl.pallas_call(
        functools.partial(finish_kernel, heads, key, val, len(wait)),
        grid=(steps,),
        in_specs=[
            pl.BlockSpec(memory_space=pltpu.SMEM),
            row(raw),
            pl.BlockSpec((HALO, width), lambda i: (jnp.maximum((steps - 1 - i) * ratio - 1, 0), 0)),
            whole(taps),
            whole(rates),
        ] + [row(a) for a in given] + [states, states] + [pl.BlockSpec(memory_space=pl.ANY)] * len(wait),
        out_specs=[out_row(wide), out_row(LANES), out_row(every), fixed((8, wide)), fixed((8, LANES))],
        out_shape=[*(jax.ShapeDtypeStruct((length, w), BF16) for w in (wide, LANES, every)), jax.ShapeDtypeStruct((8, wide), F32),
              jax.ShapeDtypeStruct((8, LANES), F32)],
        scratch_shapes=[pltpu.VMEM((ROWS + HALO, wide), F32)],
        compiler_params=params(),
        cost_estimate=cost(0.1),
        name="finish",
    )(lengths, raw, raw, taps, rates, *given, enter, leave, *wait)


def rows_kernel(order_ref, gain_ref, thin_ref, *refs):
    pieces, (normed_ref, logits_ref) = refs[:-2], refs[-2:]
    order, size = order_ref[...], pieces[0].shape[0]
    token = iota((order.shape[0], size), 1)
    rows = sum(
        jnp.dot((order == token + i * size).astype(BF16), piece[...], preferred_element_type=F32)
        for i, piece in enumerate(pieces)
    )
    scale = lax.rsqrt(lane_sum(rows * rows) * (1.0 / rows.shape[1]) + EPS)
    normed = (rows * scale * gain_ref[...]).astype(BF16)
    normed_ref[...] = normed
    logits_ref[...] = mm_bt(normed, thin_ref[...]).astype(BF16)


def packed_rows(order, gain, thin, pieces):
    length, size, wide = order.shape[0], 256, gain.shape[1]
    row = lambda w: pl.BlockSpec((size, w), lambda i: (i, 0))
    whole = lambda a: pl.BlockSpec(a.shape, lambda i: (0, 0))
    return pl.pallas_call(
        rows_kernel,
        grid=(length // size,),
        in_specs=[row(1), whole(gain), whole(thin)] + [whole(p) for p in pieces],
        out_specs=[row(wide), row(LANES)],
        out_shape=[jax.ShapeDtypeStruct((length, w), BF16) for w in (wide, LANES)],
        compiler_params=params(),
        cost_estimate=cost(26),
        name="packed_rows",
    )(order, gain, thin, *pieces)


def hidden_kernel(rows_ref, gate_ref, up_ref, grad_ref, act_ref, both_ref):
    rows = rows_ref[...]
    gating = jnp.dot(rows, gate_ref[...], preferred_element_type=F32)
    up = jnp.dot(rows, up_ref[...], preferred_element_type=F32)
    sig = 1.0 / (1.0 + jnp.exp(-gating))
    silu = gating * sig
    grad = grad_ref[...]
    act_ref[...] = (silu * up).astype(BF16)
    ggate = (grad * up * (sig + silu * (1.0 - sig))).astype(BF16)
    gup = (grad * silu).astype(BF16)
    both_ref[:, : ggate.shape[1]] = ggate
    both_ref[:, ggate.shape[1] :] = gup


def hidden_units(rows, gate, up, grad):
    (length, wide), units, size = rows.shape, gate.shape[1], 256
    row = lambda w: pl.BlockSpec((size, w), lambda i: (i, 0))
    weight = pl.BlockSpec(gate.shape, lambda i: (0, 0))
    return pl.pallas_call(
        hidden_kernel,
        grid=(length // size,),
        in_specs=[row(wide), weight, weight, row(units)],
        out_specs=[row(units), row(2 * units)],
        out_shape=[jax.ShapeDtypeStruct((length, w), BF16) for w in (units, 2 * units)],
        compiler_params=params(),
        cost_estimate=cost(0.1),
        name="hidden_units",
    )(rows, gate, up, grad)


def in_vmem(count):
    return [pl.BlockSpec(memory_space=pltpu.VMEM)] * count


def deal_kernel(n_parts, at, *refs):
    parts, outs = refs[:n_parts], refs[n_parts:]
    for d, out in enumerate(outs):
        for c in range(len(outs)):

            @pl.when((at[0] ^ d) == c)
            def _(out=out, c=c):
                begin = 0
                for part in parts:
                    width = part.shape[1] // len(outs)
                    out[:, begin : begin + width] = part[:, c * width : (c + 1) * width]
                    begin += width


def deal(at, parts, count):
    rows, width = parts[0].shape[0], sum(p.shape[1] for p in parts) // count
    return pl.pallas_call(
        functools.partial(deal_kernel, len(parts)),
        in_specs=[pl.BlockSpec(memory_space=pltpu.SMEM)] + in_vmem(len(parts)),
        out_specs=in_vmem(count),
        out_shape=[jax.ShapeDtypeStruct((rows, width), BF16)] * count,
        cost_estimate=cost(3),
        name="deal",
    )(at, *parts)


def stack_kernel(count, at, *refs):
    blocks, outs, rows = refs[:count], refs[count:], refs[0].shape[0]
    for d, block in enumerate(blocks):
        begin = 0
        for out in outs:
            width = out.shape[1]
            out[pl.ds(pl.multiple_of((at[0] ^ d) * rows, rows), rows), :] = block[:, begin : begin + width]
            begin += width


def stack(at, blocks, widths):
    rows = blocks[0].shape[0]
    return pl.pallas_call(
        functools.partial(stack_kernel, len(blocks)),
        in_specs=[pl.BlockSpec(memory_space=pltpu.SMEM)] + in_vmem(len(blocks)),
        out_specs=in_vmem(len(widths)),
        out_shape=[jax.ShapeDtypeStruct((len(blocks) * rows, w), BF16) for w in widths],
        cost_estimate=cost(2),
        name="stack",
    )(at, *blocks)


def collect_kernel(count, n_wait, at, *refs):
    blocks, outs = refs[:count], refs[count + n_wait :]
    for d, block in enumerate(blocks):
        for c in range(count):

            @pl.when((at[0] ^ d) == c)
            def _(block=block, c=c):
                begin = 0
                for out in outs:
                    width = out.shape[1] // count
                    out[:, c * width : (c + 1) * width] = block[:, begin : begin + width].astype(F32)
                    begin += width


def collect(at, blocks, widths, wait=()):
    rows, count = blocks[0].shape[0], len(blocks)
    return pl.pallas_call(
        functools.partial(collect_kernel, count, len(wait)),
        in_specs=[pl.BlockSpec(memory_space=pltpu.SMEM)] + in_vmem(count)
        + [pl.BlockSpec(memory_space=pl.ANY)] * len(wait),
        out_specs=in_vmem(len(widths)),
        out_shape=[jax.ShapeDtypeStruct((rows, w * count), F32) for w in widths],
        compiler_params=pltpu.CompilerParams(vmem_limit_bytes=32 * 2**20),
        cost_estimate=cost(2),
        name="collect",
    )(at, *blocks, *wait)


def tie_kernel(*refs):
    del refs


def tie(value, *earlier):
    anywhere = pl.BlockSpec(memory_space=pl.ANY)
    return pl.pallas_call(
        tie_kernel,
        in_specs=[anywhere] * (1 + len(earlier)),
        out_specs=anywhere,
        out_shape=jax.ShapeDtypeStruct(value.shape, value.dtype),
        input_output_aliases={0: 0},
        cost_estimate=cost(0.3),
        name="tie",
    )(value, *earlier)


def divide_kernel(count, at, *refs):
    parts, outs, rows = refs[:-count], refs[-count:], refs[-1].shape[0]
    for d, out in enumerate(outs):
        begin = 0
        for part in parts:
            width = part.shape[1]
            out[:, begin : begin + width] = part[pl.ds(pl.multiple_of((at[0] ^ d) * rows, rows), rows), :]
            begin += width


def divide(at, parts, count):
    rows, width = parts[0].shape[0] // count, sum(p.shape[1] for p in parts)
    return pl.pallas_call(
        functools.partial(divide_kernel, count),
        in_specs=[pl.BlockSpec(memory_space=pltpu.SMEM)] + in_vmem(len(parts)),
        out_specs=in_vmem(count),
        out_shape=[jax.ShapeDtypeStruct((rows, width), BF16)] * count,
        compiler_params=pltpu.CompilerParams(vmem_limit_bytes=32 * 2**20),
        cost_estimate=cost(3),
        name="divide",
    )(at, *parts)


def dense(a, b):
    return jnp.dot(a, b, preferred_element_type=F32)


def dense_t(a, b):
    return lax.dot_general(a, b, (((0,), (0,)), ((), ())), preferred_element_type=F32)


def dense_bt(a, b):
    return lax.dot_general(a, b, (((1,), (1,)), ((), ())), preferred_element_type=F32)


def flip(axis, distance, size):
    return lambda a: lax.ppermute(a, axis, [(i, i ^ distance) for i in range(size)])


def after(value, *earlier):
    return lax.optimization_barrier((value, *earlier))[0]


def local(
    residual, cotangent, lengths, token_order, norm_mixer, w_query, w_key, w_value, w_outgate, w_decay, w_beta,
    conv_query, conv_key, conv_value, decay_log, decay_bias, norm_head, w_output, norm_ffn, w_gate, w_up, w_down,
):
    n_ctx, n_tp = lax.axis_size("ctx"), lax.axis_size("tp")
    at_ctx, at_tp = lax.axis_index("ctx"), lax.axis_index("tp")
    rows_d = w_query.shape[0]
    heads = w_decay.shape[1] // n_ctx
    key = w_query.shape[1] // (n_ctx * heads)
    val = w_value.shape[1] // (n_ctx * heads)
    hk, hv = heads * key, heads * val
    wide = 2 * hk + hv
    units = w_gate.shape[1] // n_ctx
    group = token_order.shape[1]
    mine = group // (n_ctx * n_tp)

    across_core, across_x = flip("ctx", 1, n_ctx), flip("ctx", 2, n_ctx)
    across_both, across_y = flip("ctx", 3, n_ctx), flip("tp", 1, n_tp)
    half = mine // 2
    at_x, at_core = at_ctx // 2, at_ctx % 2

    def place_of(token):
        part, rest = token // half, token % half
        second, other_y = part % 2, (part // 2 % 2) ^ at_tp
        other_core, other_x = (part // 4 % 2) ^ at_core, (part // 8) ^ at_x
        pair = jnp.where(second == 1, other_y * 2 + other_x, other_x * 2 + other_y)
        return ((other_core * 2 + second) * 4 + pair) * half + rest

    def beside(*transfers):
        return lax.optimization_barrier(transfers)

    def place_given(token):
        part = (at_ctx ^ (token // (2 * mine)))
        return ((part % 2) * 2 + part // 2) * (2 * mine) + token % (2 * mine)

    def gather_tokens(block):
        first, second = block[:half], block[half:]
        first_y, second_x = beside(across_y(first), across_x(second))
        first = jnp.concatenate([first, first_y], axis=0)
        second = jnp.concatenate([second, second_x], axis=0)
        first_x, second_y = beside(across_x(first), across_y(second))
        chip = (first, first_x, second, second_y)
        return jnp.concatenate([*chip, *(across_core(piece) for piece in chip)], axis=0)

    def sort_given(near, far):
        def pick(block, second, other):
            return lax.dynamic_slice_in_dim(block, (at_tp ^ other) * mine + second * half, half, 0)

        def chip(near, far):
            return [
                *(pick(b, 0, other) for b in (near, far) for other in (0, 1)),
                *(pick(b, 1, other) for other in (0, 1) for b in (near, far)),
            ]

        return jnp.concatenate(chip(near, far) + chip(across_core(near), across_core(far)), axis=0)

    def product(*pairs):
        size = pairs[0][0].shape[0] // 4
        return [
            sum(dense_bt(rows[i * size : (i + 1) * size], matrix) for rows, matrix in pairs).astype(BF16)
            for i in (2, 3, 0, 1)
        ]

    def sum_cores(theirs_first, theirs_second, first, second):
        theirs_first, theirs_second = across_core(theirs_first), across_core(theirs_second)
        near, far = slice(0, 2 * half), slice(2 * half, 4 * half)
        return (
            both(first[near], theirs_first[near]), both(second[near], theirs_second[near]),
            both(first[far], theirs_first[far]).astype(BF16), both(second[far], theirs_second[far]).astype(BF16),
        )

    def sum_near(first, second, far_first, far_second):
        moved_first, moved_second = beside(across_x(far_first), across_y(far_second))
        first, second = both(first, moved_first), both(second, moved_second)
        return first[:half], second[:half], first[half:].astype(BF16), second[half:].astype(BF16)

    def sum_far(first, second, moved_first, moved_second):
        moved_first, moved_second = beside(across_y(moved_first), across_x(moved_second))
        return jnp.concatenate([both(first, moved_first), both(second, moved_second)], axis=0)

    def sum_tokens(*parts):
        return sum_far(*sum_near(*sum_cores(*parts)))

    def both(a, b):
        return a.astype(F32) + b.astype(F32)

    def pair_tokens(block):
        return order_pair(block, across_y(block))

    def order_pair(block, other):
        return jnp.where(
            at_tp == 0, jnp.concatenate([block, other], axis=0), jnp.concatenate([other, block], axis=0)
        )

    at_here = jnp.reshape(at_ctx, (1,)).astype(jnp.int32)

    def exchange(blocks):
        return [blocks[0], across_core(blocks[1]), across_x(blocks[2]), across_both(blocks[3])]

    def spread(place, *parts):
        blocks = exchange(deal(place, parts, n_ctx))
        return stack(at_here, blocks, (blocks[0].shape[1],))[0]

    def every(block):
        return lax.all_gather(block, "fsdp", axis=0, tiled=True)

    def reduce(partial):
        return lax.psum_scatter(partial, "fsdp", scatter_dimension=0, tiled=True)

    def own(place, blocks, *widths):
        return collect(at_here, exchange(divide(place, blocks, n_ctx)), widths)

    def vectors(block):
        n_groups, count, distance = lax.axis_size("fsdp"), block.shape[0], 1
        places = []
        for move, place in ((across_core, at_core), (across_x, at_x)):
            block, places = jnp.stack([block, move(block)]), [place, *places]
        while distance < n_groups:
            block = jnp.stack([block, flip("fsdp", distance, n_groups)(block)])
            places = [lax.axis_index("fsdp") // distance % 2, *places]
            distance *= 2
        moved = block
        for axis, place in enumerate(places):
            block = jnp.where(place == 0, block, jnp.flip(block, axis))
        return jnp.moveaxis(block.reshape(-1, count, block.shape[-1]), 1, 0).reshape(count, -1), moved

    first_in = spread(at_here, w_query, w_key, w_value)
    w_first = every(first_in)
    thin, thin_moved = vectors(jnp.concatenate([norm_mixer[None], norm_ffn[None], w_decay.T, w_beta.T], axis=0))
    n_mix, n_ffn = thin[0].astype(F32), thin[1].astype(F32)
    w_thin = jnp.concatenate([
        lax.dynamic_slice_in_dim(thin, 2 + at_ctx * heads, heads, 0),
        lax.dynamic_slice_in_dim(thin, 2 + (n_ctx + at_ctx) * heads, heads, 0),
    ])
    w_thin = jnp.pad(w_thin, ((0, LANES - 2 * heads), (0, 0)))
    source_in = lax.dynamic_slice_in_dim(residual, at_tp * mine, mine, 0)
    near = tie(residual, first_in, thin_moved)
    far = across_x(near)
    tokens = (near, far, across_core(near), across_core(far))
    order = place_of(token_order[0])
    inverse = jnp.zeros_like(order).at[order].set(lax.iota(jnp.int32, group))
    second_in = spread(tie(at_here, far, thin, inverse), w_outgate, w_output.T)
    w_second = every(second_in)
    w_gates, w_out = w_second[:, :hv], w_second[:, hv:]
    normed1, raw_thin = packed_rows(place_given(token_order[0])[:, None], n_mix[None], w_thin, tokens)
    cot_in = lax.dynamic_slice_in_dim(cotangent, at_tp * mine, mine, 0)
    raw = dense(normed1, w_first).astype(BF16)
    cot_far = across_x(tie(cotangent, raw))
    cot = sort_given(cotangent, cot_far)
    later = tie(at_here, raw)
    last_in, gate_in, up_in = spread(later, w_down.T), spread(later, w_gate), spread(later, w_up)
    w_last, w_gating, w_uppart = every(last_in), every(gate_in), every(up_in)

    first_head = (at_tp * n_ctx + at_ctx) * heads

    def share(conv, width):
        return lax.dynamic_slice_in_dim(conv.astype(F32), first_head * width, heads * width, 1)

    taps = jnp.concatenate([share(conv_query, key), share(conv_key, key), share(conv_value, val)], axis=1)
    taps = jnp.concatenate([taps, jnp.zeros_like(taps)], axis=0)
    rates = jnp.stack([
        lax.dynamic_slice_in_dim(decay_log, first_head, heads, 0),
        lax.dynamic_slice_in_dim(decay_bias, first_head, heads, 0),
    ])
    rates = jnp.pad(rates, ((0, 6), (0, LANES - heads)))
    gain = norm_head.astype(F32)[None, :]
    sizes = (heads, key, val)
    u, qe, wm, kd, fresh, p, solve, decay, gram, cols = prepare(
        raw, raw_thin, taps, rates, lengths, *sizes, wait=(second_in,)
    )
    headout, mixed, new, gate, enter = forward(
        qe, wm, kd, fresh, p, cols, normed1, w_second, gain, *sizes, wait=(last_in, gate_in)
    )

    given = headout[tie(inverse, cot_far, up_in)]
    attention = sum_tokens(*product((given, w_out)))
    source = source_in.astype(F32)
    middle = source + attention
    scale2 = lax.rsqrt(jnp.mean(middle * middle, axis=-1, keepdims=True) + EPS)
    grad_act = dense(cot, w_last)
    normed2 = (middle * scale2 * n_ffn).astype(BF16)
    normed2 = gather_tokens(tie(normed2, grad_act, w_gating))
    w_hidden = jnp.concatenate([w_gating, w_uppart], axis=1)
    activation, grad_hidden = hidden_units(normed2, w_gating, w_uppart, grad_act)
    g_last = dense_t(cot, activation).astype(BF16)
    grad_hidden = tie(grad_hidden, g_last)
    g_last = reduce(g_last)
    grad_parts = product((grad_hidden, w_hidden))
    grad_normed2 = sum_tokens(*grad_parts)
    g_hidden = dense_t(tie(normed2, *grad_parts), grad_hidden).astype(BF16)

    def norm_back(u_in, s, n, g):
        weighted = n * g
        return s * weighted - u_in * (s * s * s) * jnp.mean(u_in * weighted, axis=-1, keepdims=True)

    grad_mid = cot_in.astype(F32) + norm_back(middle, scale2, n_ffn, grad_normed2)
    ffn_parts = product((activation, w_last))
    w_all = jnp.concatenate([w_first, w_gates, w_thin.T], axis=1)
    grad_attn = gather_tokens(tie(grad_mid.astype(BF16), *ffn_parts, g_hidden, g_last, w_all))
    g_hidden = reduce(g_hidden)
    grad_given = dense(grad_attn, w_out).astype(BF16)

    ffn_send = sum_cores(tie(ffn_parts[0], grad_attn), tie(ffn_parts[1], grad_attn), *ffn_parts[2:])
    ffn_near = sum_near(*ffn_send)
    grad_gate, g_gain, do, dn, leave = backward(
        grad_given[tie(order, ffn_send[2], ffn_send[3])], mixed, gate, gain, p, qe, wm, kd, cols, *sizes
    )
    g_out = reduce(dense_t(grad_attn, tie(given, grad_gate)).astype(BF16))
    g_gates = dense_t(normed1, grad_gate).astype(BF16)
    ffn_out = sum_far(*ffn_near)
    dx, dx_thin, dx_all, g_taps, g_small = finish(
        raw, taps, rates, lengths, u, p, solve, decay, gram, cols, new, do, dn, grad_gate, enter, leave, *sizes,
        wait=(g_gates, *ffn_near[2:], g_hidden),
    )
    g_gates = reduce(g_gates)
    output = (middle + ffn_out).astype(BF16)
    output_other = across_y(output)
    output = order_pair(output, output_other)
    gw_gate, gw_up, gw_down = collect(
        at_here, exchange(divide(at_here, (g_hidden, g_last), n_ctx)), (units, units, units), wait=(output_other,)
    )
    g_first = dense_t(normed1, tie(dx, ffn_out)).astype(BF16)
    inverse = tie(inverse, g_first, g_out, g_gates)
    g_first = reduce(g_first)
    grad_parts = product((tie(dx_all[inverse], output, gw_gate), w_all))
    grad_near = sum_near(*sum_cores(*grad_parts))
    grad_near = (*grad_near[:2], tie(grad_near[2], g_first), grad_near[3])
    grad_normed1 = sum_far(*grad_near)
    scale1 = lax.rsqrt(jnp.mean(source * source, axis=-1, keepdims=True) + EPS)
    grad_input = (grad_mid + norm_back(source, scale1, n_mix, grad_normed1)).astype(BF16)
    g_taps = tie(g_taps, *grad_parts)
    later, other = tie(at_here, grad_normed1), across_y(grad_input)
    grad_input = order_pair(grad_input, other)

    gw_query, gw_key, gw_value, gw_output, gw_outgate = collect(
        at_here, exchange(divide(later, (g_first, g_out, g_gates), n_ctx)), (hk, hk, hv, hv, hv), wait=(other,)
    )
    gw_output, gw_down = gw_output.T, gw_down.T

    def pad(vector):
        return jnp.pad(vector, (0, -vector.size % LANES)).reshape(-1, LANES)

    g_thin = dense_t(dx_thin, normed1)[: 2 * heads].reshape(-1, LANES)
    sums = jnp.concatenate([g_taps[:TAPS].reshape(-1, LANES), pad(g_gain[0]), g_small[:2], g_thin], axis=0)
    n_groups, distance = lax.axis_size("fsdp"), 1
    while distance < n_groups:
        sums = sums + flip("fsdp", distance, n_groups)(sums)
        distance *= 2
    for move in (across_y, across_x, across_core):
        sums = jnp.stack([sums, move(sums)])
    sums = sums.reshape(2, 2, 2, *sums.shape[3:])
    sums = jnp.where(at_core == 0, sums, sums[::-1])
    sums = jnp.where(at_x == 0, sums, sums[:, ::-1])
    sums = jnp.where(at_tp == 0, sums, sums[:, :, ::-1])
    sums = sums.transpose(2, 1, 0, 3, 4).reshape(n_tp * n_ctx, *sums.shape[3:])
    of_taps = TAPS * wide // LANES
    of_thin = g_thin.shape[0]
    tap_sums = sums[:, :of_taps].reshape(-1, TAPS, wide).swapaxes(0, 1)

    def heads_of(begin, end):
        return tap_sums[:, :, begin:end].reshape(TAPS, -1)

    pieces = (
        heads_of(0, hk), heads_of(hk, 2 * hk), heads_of(2 * hk, wide),
        sums[:, -2 - of_thin, :heads].reshape(-1), sums[:, -1 - of_thin, :heads].reshape(-1),
        jnp.sum(sums[:, of_taps : -2 - of_thin], axis=0).reshape(-1)[:val],
    )
    thin_sums = sums[:, -of_thin:].reshape(n_tp, n_ctx, 2, heads, n_ctx * lax.axis_size("fsdp"), rows_d)
    thin_sums = lax.dynamic_index_in_dim(thin_sums, at_tp, 0, keepdims=False)
    thin_sums = lax.dynamic_index_in_dim(thin_sums, lax.axis_index("fsdp") * n_ctx + at_ctx, 3, keepdims=False)
    gw_decay = thin_sums[:, 0].reshape(-1, rows_d).T
    gw_beta = thin_sums[:, 1].reshape(-1, rows_d).T

    def overlap(*pairs):
        return sum(jnp.sum(w.astype(F32) * g, axis=1) for w, g in pairs)

    g_norms = jnp.stack([
        overlap((w_query, gw_query), (w_key, gw_key), (w_value, gw_value), (w_outgate, gw_outgate),
                (w_decay, gw_decay), (w_beta, gw_beta)) / norm_mixer.astype(F32),
        overlap((w_gate, gw_gate), (w_up, gw_up)) / norm_ffn.astype(F32),
    ])
    g_norms = g_norms + across_y(g_norms)

    return (
        output, grad_input, g_norms[0], gw_query, gw_key, gw_value, gw_outgate, gw_decay, gw_beta,
        *pieces, gw_output, g_norms[1], gw_gate, gw_up, gw_down,
    )


def solution(mesh):
    rows = ("fsdp", "ctx")
    up, down, vector, copied = P(rows, "tp"), P("tp", rows), P(rows), P()
    in_specs = (
        P(rows, None), P(rows, None), P("fsdp", None), P("fsdp", None), vector, up, up, up, up, up, up,
        copied, copied, copied, copied, copied, copied, down, vector, up, up, down,
    )
    out_specs = (
        P(rows, None), P(rows, None), vector, up, up, up, up, up, up,
        copied, copied, copied, copied, copied, copied, down, vector, up, up, down,
    )
    return jax.shard_map(local, mesh=mesh, in_specs=in_specs, out_specs=out_specs, check_vma=False)
```
